32 devices in a mesh: row: 4 (over y, core), col: 8 (over z, x).
Axes of the slice: x: 2, y: 2, z: 4, core: 2. Of those that a mesh axis runs over, the one named last changes fastest.
Arguments:
- grad: bfloat16 [8192, 4096], P('row', 'col'), may hold values from -6 to 6
- basis_left: bfloat16 [8192, 8192], P('row', 'col'), may hold values from -0.0625 to 0.0625
- basis_right: bfloat16 [4096, 4096], P('row', 'col'), may hold values from -0.09375 to 0.09375
- first_moment: float32 [8192, 4096], P('col', 'row'), may hold values from -6 to 6
- second_moment: float32 [8192, 4096], P('col', 'row'), may hold values from 0.25 to 4
Outputs:
- update: bfloat16 [8192, 4096], P('row', 'col')
- first_new: float32 [8192, 4096], P('col', 'row')
- second_new: float32 [8192, 4096], P('col', 'row')
The draws below stay inside these ranges and needn't reach their ends.
All inputs are finite; a program needn't handle non-finite values.
Results may differ from the reference program's by a relative error of at most 0.029.
Values may be sent and summed in bfloat16 or wider, within the bound.
No kernel may reach another device: no remote copies, remote signals or barrier semaphores. Data moves between devices by JAX's collectives and lax.ppermute only.
A program may use at most 128 MiB of HBM per device.

```python
import math
import jax
import jax.numpy as jnp
from jax import lax

M = 8192
NB = 4096
N_ROW = 4
N_COL = 8


def block_levels(stream_key, shape, cuts, low, largest):
    factor_of = 1.0
    for dim, shards_of in cuts:
        draws = jax.random.uniform(jax.random.fold_in(jax.random.fold_in(stream_key, 6), dim), (shards_of,), jnp.float32, low / len(cuts), largest / len(cuts))
        factor_of = factor_of * jnp.repeat(jnp.exp(draws), shape[dim] // shards_of).reshape((-1,) + (1,) * (len(shape) - 1 - dim))
    return factor_of


def scatter_about(stream_key, shape, spread, reach, shards=(), kind=jnp.bfloat16):
    loudness = block_levels(stream_key, shape, shards, -0.22, 0.18) if shards else 1.0
    array = jax.random.normal(stream_key, shape, jnp.float32) * spread * loudness
    return jnp.minimum(jnp.maximum(array, -reach), reach).astype(kind)


def setup_inputs(seed: int = 0) -> dict:
    key_list = jax.random.split(jax.random.key(seed), 6)
    grad = scatter_about(key_list[0], (M, NB), 1.0, 6.0, ((0, 4), (1, 8)))
    basis_left = scatter_about(key_list[1], (M, M), M ** -0.5, 0.0625, ((0, 4), (1, 8)))
    basis_right = scatter_about(key_list[2], (NB, NB), NB ** -0.5, 0.09375, ((0, 4), (1, 8)))
    first_moment = scatter_about(key_list[3], (M, NB), 1.0, 6.0, ((0, 8), (1, 4)), jnp.float32)
    second_moment = jnp.clip(jnp.exp(math.log(4.0) - 2.7725887 * jax.random.uniform(key_list[4], (M, NB), jnp.float32) ** block_levels(key_list[4], (M, NB), ((0, 8), (1, 4)), -0.2, 0.2)), 0.25, 4.0)
    return dict(grad=grad, basis_left=basis_left, basis_right=basis_right, first_moment=first_moment, second_moment=second_moment)


def rounded_sum(pairs):
    total = None
    for left_part, right_part in pairs:
        product = jnp.dot(left_part, right_part, preferred_element_type=jnp.float32)
        product = lax.optimization_barrier(product.astype(jnp.bfloat16)).astype(jnp.float32)
        total = product if total is None else total + product
    return total

def reference(grad, basis_left, basis_right, first_moment, second_moment):
    row_block = M // N_ROW
    left_rotated = rounded_sum([(basis_left[b * row_block:(b + 1) * row_block, :].T, grad[b * row_block:(b + 1) * row_block, :]) for b in range(N_ROW)]).astype(jnp.bfloat16)
    col_block = NB // N_ROW
    rotated = rounded_sum([(left_rotated[:, b * col_block:(b + 1) * col_block], basis_right[b * col_block:(b + 1) * col_block, :]) for b in range(N_ROW)])
    first_new = 0.9 * first_moment + 0.1 * rotated
    second_new = 0.95 * second_moment + 0.05 * rotated * rotated
    direction = (first_new / (jnp.sqrt(second_new) + 1e-08)).astype(jnp.bfloat16)
    inner_block = M // N_COL
    back_left = rounded_sum([(basis_left[:, b * inner_block:(b + 1) * inner_block], direction[b * inner_block:(b + 1) * inner_block, :]) for b in range(N_COL)]).astype(jnp.bfloat16)
    last_block = NB // N_COL
    update = rounded_sum([(back_left[:, b * last_block:(b + 1) * last_block], basis_right[:, b * last_block:(b + 1) * last_block].T) for b in range(N_COL)]).astype(jnp.bfloat16)
    return (update, first_new, second_new)
```

```python
import jax
import jax.numpy as jnp
from jax import lax
from jax.sharding import PartitionSpec as P

BF16 = jnp.bfloat16
F32 = jnp.float32


def dot(a, b, contract):
    return lax.dot_general(a, b, ((contract[:1], contract[1:]), ((), ())), preferred_element_type=F32)


def solution(mesh):
    n_row, n_col = mesh.shape["row"], mesh.shape["col"]
    n_a = 4 if n_col % 4 == 0 else n_col
    n_b = n_col // n_a
    per_row = n_col // n_row

    def col_shift(x, da, db):
        perm = [
            (a * n_b + b, ((a + da) % n_a) * n_b + (b + db) % n_b)
            for a in range(n_a)
            for b in range(n_b)
        ]
        return lax.ppermute(x, "col", perm)

    def row_xor(x, k):
        return lax.ppermute(x, "row", [(r, r ^ k) for r in range(n_row)])

    def half_sum(theirs, mine_f32):
        got = row_xor(theirs.astype(BF16), 1)
        mine = (mine_f32 + got.astype(F32)).astype(BF16)
        k = 2
        while k < n_row:
            mine = (mine.astype(F32) + row_xor(mine, k).astype(F32)).astype(BF16)
            k *= 2
        return mine, row_xor(mine, 1)

    def per_device(grad, basis_left, basis_right, first_moment, second_moment):
        r = lax.axis_index("row")
        c = lax.axis_index("col")
        a, b = c // n_b, c % n_b
        core = r % 2
        width = grad.shape[1]
        half = width // 2
        sub = width // n_row
        own_i = basis_left.shape[1]

        lefts = [basis_left] + [col_shift(basis_left, 0, -k) for k in range(1, n_b)]
        left = jnp.concatenate(lefts, axis=1)

        g_theirs = lax.dynamic_slice_in_dim(grad, (1 - core) * half, half, 1)
        g_mine = lax.dynamic_slice_in_dim(grad, core * half, half, 1)
        pieces = []
        for s in range(n_a):
            if s:
                g_theirs, g_mine = col_shift(g_theirs, 1, 0), col_shift(g_mine, 1, 0)
            pieces += half_sum(dot(left, g_theirs, (0, 0)), dot(left, g_mine, (0, 0)))
        left_rotated = jnp.concatenate(pieces, axis=1)

        right_all = lax.all_gather(basis_right, "row", axis=0, tiled=True)
        right_all = lax.dynamic_slice_in_dim(right_all, r * sub, sub, 1)
        by_b = right_all.reshape(n_a, n_b, width, sub)

        def rows_of(which):
            return lax.dynamic_index_in_dim(by_b, which, 1, keepdims=False).reshape(n_a * width, sub)

        got = [rows_of(b)] + [col_shift(rows_of((b + k) % n_b), 0, k) for k in range(1, n_b)]
        stacked = jnp.stack(got, 0)
        right_s = jnp.concatenate(
            [lax.dynamic_index_in_dim(stacked, (b - q) % n_b, 0, keepdims=False) for q in range(n_b)], axis=1
        )

        def relative(x):
            parts = []
            for s in range(n_a):
                start = ((a - s) % n_a) * width
                parts.append(lax.dynamic_slice_in_dim(x, start + core * half, half, 0))
                parts.append(lax.dynamic_slice_in_dim(x, start + (1 - core) * half, half, 0))
            return jnp.concatenate(parts, axis=0)

        rights, rots = [], []
        for t in range(n_a):
            if t:
                right_s = col_shift(right_s, 1, 0)
            right_t = relative(right_s)
            rights.append(right_t)
            rot = dot(left_rotated[:own_i], right_t, (1, 0))
            for k in range(1, n_b):
                part = dot(left_rotated[k * own_i : (k + 1) * own_i], right_t, (1, 0))
                rot = rot + col_shift(part.astype(BF16), 0, k).astype(F32)
            rots.append(rot.astype(BF16))

        def in_order(parts):
            stacked = jnp.stack(parts, 0)
            return jnp.concatenate(
                [lax.dynamic_index_in_dim(stacked, (a - q) % n_a, 0, keepdims=False) for q in range(n_a)], axis=1
            )

        rot_cols = in_order(rots)
        right_cols = in_order(rights)
        piece = per_row * sub

        first_new, second_new = first_moment, second_moment
        directions, right_k = [], []
        for k in range(n_row):
            peer = r ^ k
            rot = lax.dynamic_slice_in_dim(rot_cols, peer * piece, piece, 1)
            right_k.append(lax.dynamic_slice_in_dim(right_cols, peer * piece, piece, 1))
            if k:
                rot = row_xor(rot, k)
            rot = rot.astype(F32)
            outs = []
            for q in range(per_row):
                start = (q * n_row + peer) * sub
                rot_q = rot[:, q * sub : (q + 1) * sub]
                first = 0.9 * lax.dynamic_slice_in_dim(first_moment, start, sub, 1) + 0.1 * rot_q
                second = 0.95 * lax.dynamic_slice_in_dim(second_moment, start, sub, 1) + 0.05 * rot_q * rot_q
                first_new = lax.dynamic_update_slice_in_dim(first_new, first, start, 1)
                second_new = lax.dynamic_update_slice_in_dim(second_new, second, start, 1)
                outs.append((first / (jnp.sqrt(second) + 1e-08)).astype(BF16))
            direction = jnp.concatenate(outs, axis=1)
            if k:
                direction = row_xor(direction, k)
            directions.append(direction)

        own = jnp.concatenate(directions, axis=1)
        rows = [own] + [
            jnp.concatenate([col_shift(d, 0, -k) for d in directions], axis=1) for k in range(1, n_b)
        ]
        direction = jnp.concatenate(rows, axis=0)
        right_k = jnp.concatenate(right_k, axis=1)

        u_mine = u_theirs = None
        for s in list(range(1, n_a)) + [0]:
            r_mine = right_k[s * width : s * width + half]
            r_theirs = right_k[s * width + half : (s + 1) * width]
            w_mine, w_theirs = half_sum(dot(direction, r_theirs, (1, 1)), dot(direction, r_mine, (1, 1)))
            new_mine, new_theirs = dot(left, w_mine, (1, 0)), dot(left, w_theirs, (1, 0))
            if u_mine is not None:
                new_mine = new_mine + col_shift(u_mine, 1, 0).astype(F32)
                new_theirs = new_theirs + col_shift(u_theirs, 1, 0).astype(F32)
            u_mine, u_theirs = new_mine.astype(BF16), new_theirs.astype(BF16)
        update = jnp.where(
            core == 0,
            jnp.concatenate([u_mine, u_theirs], axis=1),
            jnp.concatenate([u_theirs, u_mine], axis=1),
        )
        return update, first_new, second_new

    in_specs = (P("row", "col"), P("row", "col"), P("row", "col"), P("col", "row"), P("col", "row"))
    out_specs = (P("row", "col"), P("col", "row"), P("col", "row"))
    return jax.shard_map(per_device, mesh=mesh, in_specs=in_specs, out_specs=out_specs, check_vma=False)
```

```python
import functools

import jax
import jax.numpy as jnp
from jax import lax
from jax.experimental import pallas as pl
from jax.experimental.pallas import tpu as pltpu
from jax.sharding import PartitionSpec as P

BF16 = jnp.bfloat16
F32 = jnp.float32


def dot(a, b, contract):
    return lax.dot_general(a, b, ((contract[:1], contract[1:]), ((), ())), preferred_element_type=F32)


def tie(x, *earlier):
    return lax.optimization_barrier((x, *earlier))[0]


def moments(first, second, rot):
    first = 0.9 * first + 0.1 * rot
    second = 0.95 * second + 0.05 * rot * rot
    return first, second, (first / (jnp.sqrt(second) + 1e-08)).astype(BF16)


def moments_kernel(peer_ref, rot_ref, first_ref, second_ref, *refs):
    first_new, second_new, direction = refs[-3:]
    first_new[...], second_new[...], direction[...] = moments(
        first_ref[...], second_ref[...], rot_ref[0].astype(F32)
    )


def moments_at(peer, n_row, sub, rot, first_moment, second_moment, before):
    blocks, rows, _ = rot.shape
    block = min(rows, 512)
    packed_rot = pl.BlockSpec((1, block, sub), lambda q, i, p: (q, i, 0))
    at_peer = pl.BlockSpec((block, sub), lambda q, i, p: (i, q * n_row + p[0]))
    packed = pl.BlockSpec((block, sub), lambda q, i, p: (i, q))
    kept = [pl.BlockSpec(memory_space=pl.ANY)] * len(before)
    out = jax.ShapeDtypeStruct(first_moment.shape, F32)
    return pl.pallas_call(
        moments_kernel,
        grid_spec=pltpu.PrefetchScalarGridSpec(
            num_scalar_prefetch=1,
            grid=(blocks, rows // block),
            in_specs=[packed_rot, at_peer, at_peer] + kept,
            out_specs=[at_peer, at_peer, packed],
        ),
        out_shape=[out, out, jax.ShapeDtypeStruct((rows, blocks * sub), BF16)],
        input_output_aliases={4: 0, 5: 1} if before else {},
        cost_estimate=pl.CostEstimate(
            flops=10 * rot.size, bytes_accessed=20 * rot.size, transcendentals=2 * rot.size
        ),
    )(peer.reshape(1), rot, first_moment, second_moment, *before)


def moments_sliced(peer, n_row, sub, rot, first_moment, second_moment, before):
    first_new, second_new = before if before else (first_moment, second_moment)
    directions = []
    for q in range(rot.shape[0]):
        start = (q * n_row + peer) * sub
        first, second, direction = moments(
            lax.dynamic_slice_in_dim(first_moment, start, sub, 1),
            lax.dynamic_slice_in_dim(second_moment, start, sub, 1),
            rot[q].astype(F32),
        )
        first_new = lax.dynamic_update_slice_in_dim(first_new, first, start, 1)
        second_new = lax.dynamic_update_slice_in_dim(second_new, second, start, 1)
        directions.append(direction)
    return first_new, second_new, jnp.concatenate(directions, axis=1)


def solution(mesh):
    n_row, n_col = mesh.shape["row"], mesh.shape["col"]
    n_a = 4 if n_col % 4 == 0 else n_col
    n_b = n_col // n_a
    per_row = n_col // n_row

    def b_shift(x, db):
        perm = [(a * n_b + b, a * n_b + (b + db) % n_b) for a in range(n_a) for b in range(n_b)]
        return lax.ppermute(x, "col", perm)

    def a_shift(x, mine):
        perm = []
        for r in range(n_row):
            up = (r % 2 == 0) == mine
            for a in range(n_a):
                for b in range(n_b):
                    to = (a + (1 if up else -1)) % n_a
                    perm.append((r * n_col + a * n_b + b, r * n_col + to * n_b + b))
        return lax.ppermute(x, ("row", "col"), perm)

    def a_shift_up(x, up):
        perm = [
            (a * n_b + b, ((a + (1 if up else -1)) % n_a) * n_b + b) for a in range(n_a) for b in range(n_b)
        ]
        return lax.ppermute(x, "col", perm)

    def row_xor(x, k):
        return lax.ppermute(x, "row", [(r, r ^ k) for r in range(n_row)])

    def half_sum(theirs, mine, gate=()):
        got = row_xor(theirs().astype(BF16), 1)
        mine = (mine() + got.astype(F32)).astype(BF16)
        if gate:
            mine = tie(mine, *gate)
        k = 2
        while k < n_row:
            mine = (mine.astype(F32) + row_xor(mine, k).astype(F32)).astype(BF16)
            k *= 2
        return mine, row_xor(mine, 1)

    def per_device(grad, basis_left, basis_right, first_moment, second_moment):
        r = lax.axis_index("row")
        c = lax.axis_index("col")
        a, b = c // n_b, c % n_b
        core = r % 2
        width = grad.shape[1]
        half = width // 2
        sub = width // n_row
        own_i = basis_left.shape[1]
        row_n = basis_right.shape[0]

        def block_of(s, h):
            return (a + (2 * h - 1) * s) % n_a

        g_theirs = [lax.dynamic_slice_in_dim(grad, (1 - core) * half, half, 1)]
        g_mine = [lax.dynamic_slice_in_dim(grad, core * half, half, 1)]
        g_theirs.append(a_shift(g_theirs[0], False))
        g_mine.append(a_shift(g_mine[0], True))

        right_after = tie(basis_right, g_theirs[0], g_mine[0])
        right_n = jnp.zeros((n_row * row_n, sub), BF16)
        for k in range(n_row):
            part = lax.dynamic_slice_in_dim(right_after, (r ^ k) * sub, sub, 1)
            if k:
                part = row_xor(part, k)
            right_n = lax.dynamic_update_slice_in_dim(right_n, part, (r ^ k) * row_n, 0)
        by_b = right_n.reshape(n_a, n_b, width, sub)

        def rows_of(which):
            return lax.dynamic_index_in_dim(by_b, which, 1, keepdims=False).reshape(n_a * width, sub)

        got = [rows_of(b)] + [b_shift(rows_of((b + k) % n_b), k) for k in range(1, n_b)]

        lefts = [basis_left] + [b_shift(tie(basis_left, g_theirs[0], g_mine[0]), -k) for k in range(1, n_b)]
        lefts = list(tie(tuple(lefts), g_theirs[1], g_mine[1]))
        left = jnp.concatenate(lefts, axis=1)

        for s in range(2, n_a):
            g_theirs.append(a_shift(g_theirs[-1], False))
            g_mine.append(a_shift(g_mine[-1], True))

        got = tie(tuple(got), g_theirs[2], g_mine[2])
        stacked = jnp.stack(got, 0)
        right_b = [lax.dynamic_index_in_dim(stacked, (b - q) % n_b, 0, keepdims=False) for q in range(n_b)]
        right_up = jnp.concatenate(right_b[: n_b // 2], axis=1)
        right_down = jnp.concatenate(right_b[n_b // 2 :], axis=1)

        def n_at(s, h):
            return block_of(s, h) * width + h * half

        left_rotated = jnp.zeros((n_b * own_i, n_a * width), BF16)
        for s in range(n_a):
            mine, theirs = half_sum(
                lambda: dot(left, g_theirs[s], (0, 0)),
                lambda: dot(left, g_mine[s], (0, 0)),
            )
            left_rotated = lax.dynamic_update_slice_in_dim(left_rotated, mine, n_at(s, core), 1)
            left_rotated = lax.dynamic_update_slice_in_dim(left_rotated, theirs, n_at(s, 1 - core), 1)

        rot_k = jnp.zeros((n_col, own_i, sub), BF16)
        right_k = jnp.zeros((n_a * width, n_col * sub), BF16)
        for t in range(n_a):
            if t:
                right_up, right_down = a_shift_up(right_up, True), a_shift_up(right_down, False)
            right_t = jnp.concatenate([right_up, right_down], axis=1)
            rot = dot(left_rotated[:own_i], right_t, (1, 0))
            for k in range(1, n_b):
                part = dot(left_rotated[k * own_i : (k + 1) * own_i], right_t, (1, 0))
                rot = rot + b_shift(part.astype(BF16), k).astype(F32)
            rot = rot.astype(BF16)
            for q in range(n_b):
                block = block_of(t, 2 * q // n_b) * n_b + q
                at = (block // per_row ^ r) * per_row + block % per_row
                columns = slice(q * sub, (q + 1) * sub)
                rot_k = lax.dynamic_update_index_in_dim(rot_k, rot[:, columns], at, 0)
                right_k = lax.dynamic_update_slice_in_dim(right_k, right_t[:, columns], at * sub, 1)

        step = moments_at if sub % 128 == 0 else moments_sliced
        kept, directions = (), []
        for k in range(n_row):
            rot = rot_k[k * per_row : (k + 1) * per_row]
            if k:
                rot = row_xor(rot, k)
            *kept, direction = step(r ^ k, n_row, sub, rot, first_moment, second_moment, tuple(kept))
            if k:
                direction = row_xor(direction, k)
            directions.append(direction)
        first_new, second_new = kept

        by_rows = [directions] + [[b_shift(d, -k) for d in directions] for k in range(1, n_b)]
        by_rows = [jnp.concatenate(ds, axis=1) for ds in by_rows]

        u_mine = u_theirs = None
        gates = []
        for s in list(range(1, n_a)) + [0]:
            r_mine = lax.dynamic_slice_in_dim(right_k, n_at(s, core), half, 0)
            r_theirs = lax.dynamic_slice_in_dim(right_k, n_at(s, 1 - core), half, 0)
            new_mine = new_theirs = 0.0
            for k in range(n_b):
                w_mine, w_theirs = half_sum(
                    lambda: dot(by_rows[k], r_theirs, (1, 1)), lambda: dot(by_rows[k], r_mine, (1, 1)), gates[-2:-1]
                )
                gates.append(w_mine)
                new_mine = new_mine + dot(lefts[k], w_mine, (1, 0))
                new_theirs = new_theirs + dot(lefts[k], w_theirs, (1, 0))
            if u_mine is not None:
                new_mine = new_mine + a_shift(u_mine, True).astype(F32)
                new_theirs = new_theirs + a_shift(u_theirs, False).astype(F32)
            u_mine, u_theirs = new_mine.astype(BF16), new_theirs.astype(BF16)
        update = jnp.where(
            core == 0,
            jnp.concatenate([u_mine, u_theirs], axis=1),
            jnp.concatenate([u_theirs, u_mine], axis=1),
        )
        return update, first_new, second_new

    in_specs = (P("row", "col"), P("row", "col"), P("row", "col"), P("col", "row"), P("col", "row"))
    out_specs = (P("row", "col"), P("col", "row"), P("col", "row"))
    return jax.shard_map(per_device, mesh=mesh, in_specs=in_specs, out_specs=out_specs, check_vma=False)
```

```python
import functools

import jax
import jax.numpy as jnp
from jax import lax
from jax.experimental import pallas as pl
from jax.experimental.pallas import tpu as pltpu
from jax.sharding import PartitionSpec as P

BF16 = jnp.bfloat16
F32 = jnp.float32


def dot(a, b, contract):
    return lax.dot_general(a, b, ((contract[:1], contract[1:]), ((), ())), preferred_element_type=F32)


def tie(x, *earlier):
    return lax.optimization_barrier((x, *earlier))[0]


def moments(first, second, rot):
    first = 0.9 * first + 0.1 * rot
    second = 0.95 * second + 0.05 * rot * rot
    return first, second, (first / (jnp.sqrt(second) + 1e-08)).astype(BF16)


def moments_kernel(peer_ref, rot_ref, first_ref, second_ref, *refs):
    first_new, second_new, direction = refs[-3:]
    first_new[...], second_new[...], direction[...] = moments(
        first_ref[...], second_ref[...], rot_ref[0].astype(F32)
    )


def moments_at(peer, n_row, sub, rot, first_moment, second_moment, before):
    blocks, rows, _ = rot.shape
    block = min(rows, 512)
    packed_rot = pl.BlockSpec((1, block, sub), lambda q, i, p: (q, i, 0))
    at_peer = pl.BlockSpec((block, sub), lambda q, i, p: (i, q * n_row + p[0]))
    packed = pl.BlockSpec((block, sub), lambda q, i, p: (i, q))
    kept = [pl.BlockSpec(memory_space=pl.ANY)] * len(before)
    out = jax.ShapeDtypeStruct(first_moment.shape, F32)
    return pl.pallas_call(
        moments_kernel,
        grid_spec=pltpu.PrefetchScalarGridSpec(
            num_scalar_prefetch=1,
            grid=(blocks, rows // block),
            in_specs=[packed_rot, at_peer, at_peer] + kept,
            out_specs=[at_peer, at_peer, packed],
        ),
        out_shape=[out, out, jax.ShapeDtypeStruct((rows, blocks * sub), BF16)],
        input_output_aliases={4: 0, 5: 1} if before else {},
        cost_estimate=pl.CostEstimate(
            flops=10 * rot.size, bytes_accessed=20 * rot.size, transcendentals=2 * rot.size
        ),
    )(peer.reshape(1), rot, first_moment, second_moment, *before)


def moments_sliced(peer, n_row, sub, rot, first_moment, second_moment, before):
    first_new, second_new = before if before else (first_moment, second_moment)
    directions = []
    for q in range(rot.shape[0]):
        start = (q * n_row + peer) * sub
        first, second, direction = moments(
            lax.dynamic_slice_in_dim(first_moment, start, sub, 1),
            lax.dynamic_slice_in_dim(second_moment, start, sub, 1),
            rot[q].astype(F32),
        )
        first_new = lax.dynamic_update_slice_in_dim(first_new, first, start, 1)
        second_new = lax.dynamic_update_slice_in_dim(second_new, second, start, 1)
        directions.append(direction)
    return first_new, second_new, jnp.concatenate(directions, axis=1)


def solution(mesh):
    n_row, n_col = mesh.shape["row"], mesh.shape["col"]
    n_a = 4
    n_b = n_col // n_a
    per_row = n_col // n_row

    def b_shift(x, db):
        perm = [(a * n_b + b, a * n_b + (b + db) % n_b) for a in range(n_a) for b in range(n_b)]
        return lax.ppermute(x, "col", perm)

    def a_shift(x, mine, ahead=1):
        perm = []
        for r in range(n_row):
            by = ahead if (r % 2 == 0) == mine else -ahead
            for a in range(n_a):
                for b in range(n_b):
                    perm.append((r * n_col + a * n_b + b, r * n_col + (a + by) % n_a * n_b + b))
        return lax.ppermute(x, ("row", "col"), perm)

    def a_shift_by(x, by):
        perm = [(a * n_b + b, (a + by) % n_a * n_b + b) for a in range(n_a) for b in range(n_b)]
        return lax.ppermute(x, "col", perm)

    def row_xor(x, k):
        return lax.ppermute(x, "row", [(r, r ^ k) for r in range(n_row)])

    def per_device(grad, basis_left, basis_right, first_moment, second_moment):
        last = {}

        def in_turn(link, x, move):
            if link in last:
                x = tie(x, last[link])
            last[link] = move(x)
            return last[link]

        def across_b(x, k):
            return in_turn("b", x, lambda y: b_shift(y, k))

        def across_rows(x, k):
            return row_xor(x, k) if k == 1 else in_turn("rows", x, lambda y: row_xor(y, k))

        def half_sum(theirs, mine, arrived=()):
            got = row_xor(theirs().astype(BF16), 1)
            mine = (mine() + got.astype(F32)).astype(BF16)
            k = 2
            while k < n_row:
                got = tie(across_rows(mine, k), *arrived)
                mine = (mine.astype(F32) + got.astype(F32)).astype(BF16)
                k *= 2
            return mine, row_xor(mine, 1)

        r = lax.axis_index("row")
        c = lax.axis_index("col")
        a, b = c // n_b, c % n_b
        core = r % 2
        width = grad.shape[1]
        half = width // 2
        sub = width // n_row
        own_i = basis_left.shape[1]
        row_n = basis_right.shape[0]

        def block_of(s, h):
            return (a + (2 * h - 1) * s) % n_a

        g_theirs = [lax.dynamic_slice_in_dim(grad, (1 - core) * half, half, 1)]
        g_mine = [lax.dynamic_slice_in_dim(grad, core * half, half, 1)]
        for g, mine in ((g_theirs, False), (g_mine, True)):
            near = a_shift(g[0], mine)
            g += [near, None, a_shift(g[0], mine, -1)]

        own_left = tie(basis_left, g_theirs[0], g_mine[0])
        own_turned = lax.optimization_barrier(own_left.T)
        lefts, turned = [own_left], [own_turned]
        for k in range(1, n_b):
            lefts.append(across_b(own_left, -k))
        own_left = tie(basis_left, g_theirs[0], g_mine[0])
        own_turned = lax.optimization_barrier(own_left.T)
        lefts, turned = [own_left], [own_turned]
        for k in range(1, n_b):
            lefts.append(across_b(own_left, -k))
        right_after = tie(basis_right, g_theirs[1], g_mine[1])
        right_n = jnp.zeros((n_row * row_n, sub), BF16)
        for k in range(n_row):
            part = lax.dynamic_slice_in_dim(right_after, (r ^ k) * sub, sub, 1)
            if k:
                part = across_rows(part, k)
            right_n = lax.dynamic_update_slice_in_dim(right_n, part, (r ^ k) * row_n, 0)
        lefts = list(tie(tuple(lefts), g_theirs[1], g_mine[1], g_theirs[3], g_mine[3], right_n))
        turned += [lax.optimization_barrier(x.T) for x in lefts[1:]]
        turned = jnp.concatenate(turned, axis=0)

        by_b = right_n.reshape(n_a, n_b, width, sub)

        def rows_of(which):
            return lax.dynamic_index_in_dim(by_b, which, 1, keepdims=False).reshape(n_a * width, sub)

        got = [rows_of(b)] + [across_b(rows_of((b + k) % n_b), k) for k in range(1, n_b)]

        g_theirs[2] = a_shift(g_theirs[1], False)
        g_mine[2] = a_shift(g_mine[1], True)

        got = tie(tuple(got), g_theirs[3], g_mine[3])
        stacked = jnp.stack(got, 0)
        right_b = [lax.dynamic_index_in_dim(stacked, (b - q) % n_b, 0, keepdims=False) for q in range(n_b)]
        right_up = jnp.concatenate(right_b[: n_b // 2], axis=1)
        right_down = jnp.concatenate(right_b[n_b // 2 :], axis=1)

        def n_at(s, h):
            return block_of(s, h) * width + h * half

        ups, downs = [right_up], [right_down]
        for rights, by in ((ups, 1), (downs, -1)):
            sent = tie(rights[0], g_theirs[2], g_mine[2])
            near = a_shift_by(sent, by)
            rights += [near, a_shift_by(near, by), a_shift_by(sent, -by)]

        left_rotated = jnp.zeros((n_b * own_i, n_a * width), BF16)
        for s, arrived in ((0, ()), (1, g_theirs[2:3]), (3, ()), (2, (ups[1], downs[1]))):
            to_keep = tie(g_mine[s], *arrived)
            mine, theirs = half_sum(
                lambda: dot(turned, g_theirs[s], (1, 0)),
                lambda: dot(turned, to_keep, (1, 0)),
                (ups[3], downs[3]) if s == 2 else (),
            )
            left_rotated = lax.dynamic_update_slice_in_dim(left_rotated, mine, n_at(s, core), 1)
            left_rotated = lax.dynamic_update_slice_in_dim(left_rotated, theirs, n_at(s, 1 - core), 1)

        rot_k = jnp.zeros((n_col, own_i, sub), BF16)
        right_k = jnp.zeros((n_a * width, n_col * sub), BF16)
        swapped = []
        for t in (0, 1, 3, 2):
            right_t = jnp.concatenate(tie((ups[t], downs[t]), *swapped[-2:-1]), axis=1)
            rot = dot(left_rotated[:own_i], right_t, (1, 0))
            for k in range(1, n_b):
                part = dot(left_rotated[k * own_i : (k + 1) * own_i], right_t, (1, 0))
                swapped.append(across_b(part.astype(BF16), k))
                rot = rot + swapped[-1].astype(F32)
            rot = rot.astype(BF16)
            for q in range(n_b):
                block = block_of(t, 2 * q // n_b) * n_b + q
                at = (block // per_row ^ r) * per_row + block % per_row
                columns = slice(q * sub, (q + 1) * sub)
                rot_k = lax.dynamic_update_index_in_dim(rot_k, rot[:, columns], at, 0)
                right_k = lax.dynamic_update_slice_in_dim(right_k, right_t[:, columns], at * sub, 1)

        step = moments_at if sub % 128 == 0 else moments_sliced
        kept, directions = (), []
        for k in range(n_row):
            rot = rot_k[k * per_row : (k + 1) * per_row]
            if k:
                rot = across_rows(rot, k)
            *kept, direction = step(r ^ k, n_row, sub, rot, first_moment, second_moment, tuple(kept))
            directions.append(direction)
        first_new, second_new = kept

        by_rows = [[] for _ in range(n_b)]
        for k, direction in enumerate(directions):
            if k:
                direction = across_rows(direction, k)
            by_rows[0].append(direction)
            for q in range(1, n_b):
                by_rows[q].append(across_b(direction, -q))
        by_rows = [jnp.concatenate(ds, axis=1) for ds in by_rows]
        direction = jnp.concatenate(by_rows, axis=0)

        def back(s, parts):
            r_mine = lax.dynamic_slice_in_dim(right_k, n_at(s, core), half, 0)
            r_theirs = lax.dynamic_slice_in_dim(right_k, n_at(s, 1 - core), half, 0)
            u_mine = u_theirs = 0.0
            for d, ls in parts:
                w_mine, w_theirs = half_sum(lambda: dot(d, r_theirs, (1, 1)), lambda: dot(d, r_mine, (1, 1)))
                for k, l in enumerate(ls):
                    rows = slice(k * own_i, (k + 1) * own_i)
                    u_mine = u_mine + dot(l, w_mine[rows], (1, 0))
                    u_theirs = u_theirs + dot(l, w_theirs[rows], (1, 0))
            return u_mine, u_theirs

        far = back(2, [(d, [l]) for d, l in zip(by_rows, lefts)])
        far = [a_shift(u.astype(BF16), mine) for u, mine in zip(far, (True, False))]
        whole = [(direction, lefts)]
        behind = [a_shift(u.astype(BF16), mine, -1) for u, mine in zip(back(1, whole), (True, False))]
        ahead = lax.optimization_barrier(back(3, whole))
        ahead = [(u + f.astype(F32)).astype(BF16) for u, f in zip(ahead, far)]
        ahead = [a_shift(u, mine) for u, mine in zip(ahead, (True, False))]
        own = lax.optimization_barrier(back(0, whole))
        u_mine, u_theirs = [
            (u + x.astype(F32) + y.astype(F32)).astype(BF16) for u, x, y in zip(own, behind, ahead)
        ]
        update = jnp.where(
            core == 0,
            jnp.concatenate([u_mine, u_theirs], axis=1),
            jnp.concatenate([u_theirs, u_mine], axis=1),
        )
        return update, first_new, second_new

    in_specs = (P("row", "col"), P("row", "col"), P("row", "col"), P("col", "row"), P("col", "row"))
    out_specs = (P("row", "col"), P("col", "row"), P("col", "row"))
    return jax.shard_map(per_device, mesh=mesh, in_specs=in_specs, out_specs=out_specs, check_vma=False)
```

```python
import functools

import jax
import jax.numpy as jnp
from jax import lax
from jax.experimental import pallas as pl
from jax.experimental.pallas import tpu as pltpu
from jax.sharding import PartitionSpec as P

BF16 = jnp.bfloat16
F32 = jnp.float32


def dot(a, b, contract):
    return lax.dot_general(a, b, ((contract[:1], contract[1:]), ((), ())), preferred_element_type=F32)


def tie(x, *earlier):
    return lax.optimization_barrier((x, *earlier))[0]


def moments(first, second, rot):
    first = 0.9 * first + 0.1 * rot
    second = 0.95 * second + 0.05 * rot * rot
    return first, second, (first / (jnp.sqrt(second) + 1e-08)).astype(BF16)


def moments_kernel(peer_ref, rot_ref, first_ref, second_ref, *refs):
    first_new, second_new, direction = refs[-3:]
    first_new[...], second_new[...], direction[...] = moments(
        first_ref[...], second_ref[...], rot_ref[0].astype(F32)
    )


def moments_at(peer, n_row, sub, rot, first_moment, second_moment, before):
    blocks, rows, _ = rot.shape
    block = min(rows, 512)
    packed_rot = pl.BlockSpec((1, block, sub), lambda q, i, p: (q, i, 0))
    at_peer = pl.BlockSpec((block, sub), lambda q, i, p: (i, q * n_row + p[0]))
    packed = pl.BlockSpec((block, sub), lambda q, i, p: (i, q))
    kept = [pl.BlockSpec(memory_space=pl.ANY)] * len(before)
    out = jax.ShapeDtypeStruct(first_moment.shape, F32)
    return pl.pallas_call(
        moments_kernel,
        grid_spec=pltpu.PrefetchScalarGridSpec(
            num_scalar_prefetch=1,
            grid=(blocks, rows // block),
            in_specs=[packed_rot, at_peer, at_peer] + kept,
            out_specs=[at_peer, at_peer, packed],
        ),
        out_shape=[out, out, jax.ShapeDtypeStruct((rows, blocks * sub), BF16)],
        input_output_aliases={4: 0, 5: 1} if before else {},
        cost_estimate=pl.CostEstimate(
            flops=10 * rot.size, bytes_accessed=20 * rot.size, transcendentals=2 * rot.size
        ),
    )(peer.reshape(1), rot, first_moment, second_moment, *before)


def moments_sliced(peer, n_row, sub, rot, first_moment, second_moment, before):
    first_new, second_new = before if before else (first_moment, second_moment)
    directions = []
    for q in range(rot.shape[0]):
        start = (q * n_row + peer) * sub
        first, second, direction = moments(
            lax.dynamic_slice_in_dim(first_moment, start, sub, 1),
            lax.dynamic_slice_in_dim(second_moment, start, sub, 1),
            rot[q].astype(F32),
        )
        first_new = lax.dynamic_update_slice_in_dim(first_new, first, start, 1)
        second_new = lax.dynamic_update_slice_in_dim(second_new, second, start, 1)
        directions.append(direction)
    return first_new, second_new, jnp.concatenate(directions, axis=1)


def solution(mesh):
    n_row, n_col = mesh.shape["row"], mesh.shape["col"]
    n_a = 4
    n_b = n_col // n_a
    per_row = n_col // n_row

    def b_shift(x, db):
        perm = [(a * n_b + b, a * n_b + (b + db) % n_b) for a in range(n_a) for b in range(n_b)]
        return lax.ppermute(x, "col", perm)

    def a_shift(x, by):
        perm = [(a * n_b + b, (a + by) % n_a * n_b + b) for a in range(n_a) for b in range(n_b)]
        return lax.ppermute(x, "col", perm)

    def row_xor(x, k):
        return lax.ppermute(x, "row", [(r, r ^ k) for r in range(n_row)])

    def per_device(grad, basis_left, basis_right, first_moment, second_moment):
        last = {}

        def in_turn(link, x, move, depth):
            before = last.setdefault(link, [])
            if len(before) >= depth:
                x = tie(x, before[-depth])
            before.append(move(x))
            return before[-1]

        def across_b(x, k, depth=1):
            return in_turn("b", x, lambda y: b_shift(y, k), depth)

        def across_rows(x, k, depth=1):
            return row_xor(x, k) if k == 1 else in_turn("rows", x, lambda y: row_xor(y, k), depth)

        def half_sum(theirs, mine):
            got = row_xor(theirs().astype(BF16), 1)
            mine = (mine() + got.astype(F32)).astype(BF16)
            k = 2
            while k < n_row:
                got = across_rows(mine, k)
                mine = (mine.astype(F32) + got.astype(F32)).astype(BF16)
                k *= 2
            return mine, row_xor(mine, 1)

        r = lax.axis_index("row")
        c = lax.axis_index("col")
        a, b = c // n_b, c % n_b
        core = r % 2
        width = grad.shape[1]
        half = width // 2
        sub = width // n_row
        own_i = basis_left.shape[1]
        row_n = basis_right.shape[0]

        def n_at(s, h):
            return (a - s) % n_a * width + h * half

        def halves(x):
            return x[:, :half], x[:, half:]

        grad = jnp.concatenate(
            [lax.dynamic_slice_in_dim(grad, h * half, half, 1) for h in (core, 1 - core)], axis=1
        )
        grad = lax.optimization_barrier(grad)
        below, above = a_shift(grad, 1), a_shift(grad, -1)
        grads = [grad, below, a_shift(below, 1), above]

        own_left = tie(basis_left, grad)
        lefts = [own_left] + [across_b(own_left, -k) for k in range(1, n_b)]

        right_after = tie(basis_right, grad)
        right_n = jnp.zeros((n_row * row_n, sub), BF16)
        for k in range(n_row):
            part = lax.dynamic_slice_in_dim(right_after, (r ^ k) * sub, sub, 1)
            if k:
                part = across_rows(part, k, 2)
            right_n = lax.dynamic_update_slice_in_dim(right_n, part, (r ^ k) * row_n, 0)
        by_b = right_n.reshape(n_a, n_b, width, sub)

        def rows_of(which):
            return lax.dynamic_index_in_dim(by_b, which, 1, keepdims=False).reshape(n_a * width, sub)

        got = [rows_of(b)] + [across_b(rows_of((b + k) % n_b), k) for k in range(1, n_b)]
        stacked = jnp.stack(got, 0)
        right = [lax.dynamic_index_in_dim(stacked, (b - q) % n_b, 0, keepdims=False) for q in range(n_b)]
        right = jnp.concatenate(right, axis=1)

        near, far = (0, 1, 3), 2
        turns = [(k, s) for k in range(n_b) for s in near] + [(k, far) for k in reversed(range(n_b))]
        rotated = [jnp.zeros((own_i, n_a * width), BF16) for _ in range(n_b)]
        for k, s in turns:
            if (k, s) == (1, 0):
                lefts[1:] = tie(tuple(lefts[1:]), last["rows"][-1])
                sent = tie(right, last["rows"][-1])
                below, above = a_shift(sent, 1), a_shift(sent, -1)
                rights = [right, below, a_shift(below, 1), above]
            if (k, s) == (0, 1):
                grads[s] = tie(grads[s], right_n)
            if (k, s) in ((0, 3), (n_b - 1, far)):
                grads[s] = tie(grads[s], last["rows"][-1])
            g = grads[s]
            g_mine, g_theirs = halves(g)
            mine, theirs = half_sum(
                lambda: dot(lefts[k], g_theirs, (0, 0)), lambda: dot(lefts[k], g_mine, (0, 0))
            )
            rotated[k] = lax.dynamic_update_slice_in_dim(rotated[k], mine, n_at(s, core), 1)
            rotated[k] = lax.dynamic_update_slice_in_dim(rotated[k], theirs, n_at(s, 1 - core), 1)
        left = jnp.concatenate(lefts, axis=1)

        rot_k = jnp.zeros((n_col, own_i, sub), BF16)
        right_k = jnp.zeros((n_a * width, n_col * sub), BF16)
        swapped = []
        for t in near + (far,):
            right_t = tie(rights[t], *swapped[-2:-1])
            rot = dot(rotated[0], right_t, (1, 0))
            for k in range(1, n_b):
                part = dot(rotated[k], right_t, (1, 0))
                swapped.append(across_b(part.astype(BF16), k))
                rot = rot + swapped[-1].astype(F32)
            rot = rot.astype(BF16)
            for q in range(n_b):
                block = (a - t) % n_a * n_b + q
                at = (block // per_row ^ r) * per_row + block % per_row
                columns = slice(q * sub, (q + 1) * sub)
                rot_k = lax.dynamic_update_index_in_dim(rot_k, rot[:, columns], at, 0)
                right_k = lax.dynamic_update_slice_in_dim(right_k, right_t[:, columns], at * sub, 1)

        step = moments_at if sub % 128 == 0 else moments_sliced
        rots = [rot_k[k * per_row : (k + 1) * per_row] for k in range(n_row)]
        rots[1:] = [across_rows(rots[k], k, 2) for k in range(1, n_row)]

        kept, by_rows = (), [[] for _ in range(n_b)]
        for k, rot in enumerate(rots):
            if k >= 2:
                kept = tie(tuple(kept), by_rows[1][k - 2])
            *kept, direction = step(r ^ k, n_row, sub, rot, first_moment, second_moment, tuple(kept))
            if k:
                direction = across_rows(direction, k, 2)
            by_rows[0].append(direction)
            for q in range(1, n_b):
                by_rows[q].append(across_b(direction, -q, 2))
        first_new, second_new = kept
        by_rows = [jnp.concatenate(ds, axis=1) for ds in by_rows]
        direction = jnp.concatenate(by_rows, axis=0)

        def back(s, parts):
            r_mine = lax.dynamic_slice_in_dim(right_k, n_at(s, core), half, 0)
            r_theirs = lax.dynamic_slice_in_dim(right_k, n_at(s, 1 - core), half, 0)
            u_mine = u_theirs = 0.0
            for d, l in parts:
                w_mine, w_theirs = half_sum(lambda: dot(d, r_theirs, (1, 1)), lambda: dot(d, r_mine, (1, 1)))
                u_mine = u_mine + dot(l, w_mine, (1, 0))
                u_theirs = u_theirs + dot(l, w_theirs, (1, 0))
            return u_mine, u_theirs

        def joined(u):
            return jnp.concatenate([x.astype(BF16) for x in u], axis=1)

        whole = [(direction, left)]
        passed = halves(a_shift(joined(back(2, list(zip(by_rows, lefts)))), 1))
        behind = halves(a_shift(joined(back(1, whole)), -1))
        ahead = lax.optimization_barrier(back(3, whole))
        ahead = halves(a_shift(joined([u + x.astype(F32) for u, x in zip(ahead, passed)]), 1))
        own = lax.optimization_barrier(back(0, whole))
        u_mine, u_theirs = [
            (u + x.astype(F32) + y.astype(F32)).astype(BF16) for u, x, y in zip(own, behind, ahead)
        ]
        update = jnp.where(
            core == 0,
            jnp.concatenate([u_mine, u_theirs], axis=1),
            jnp.concatenate([u_theirs, u_mine], axis=1),
        )
        return update, first_new, second_new

    in_specs = (P("row", "col"), P("row", "col"), P("row", "col"), P("col", "row"), P("col", "row"))
    out_specs = (P("row", "col"), P("col", "row"), P("col", "row"))
    return jax.shard_map(per_device, mesh=mesh, in_specs=in_specs, out_specs=out_specs, check_vma=False)
```

```python
import functools

import jax
import jax.numpy as jnp
from jax import lax
from jax.experimental import pallas as pl
from jax.experimental.pallas import tpu as pltpu
from jax.sharding import PartitionSpec as P

BF16 = jnp.bfloat16
F32 = jnp.float32


def dot(a, b, contract):
    return lax.dot_general(a, b, ((contract[:1], contract[1:]), ((), ())), preferred_element_type=F32)


def tie(x, *earlier):
    return lax.optimization_barrier((x, *earlier))[0]


def moments(first, second, rot):
    first = 0.9 * first + 0.1 * rot
    second = 0.95 * second + 0.05 * rot * rot
    return first, second, (first / (jnp.sqrt(second) + 1e-08)).astype(BF16)


def moments_kernel(peer_ref, rot_ref, first_ref, second_ref, *refs):
    first_new, second_new, direction = refs[-3:]
    first_new[...], second_new[...], direction[...] = moments(
        first_ref[...], second_ref[...], rot_ref[0].astype(F32).T
    )


def moments_at(peer, n_row, sub, rot, first_moment, second_moment, before):
    blocks, _, rows = rot.shape
    block = min(rows, 512)
    packed_rot = pl.BlockSpec((1, sub, block), lambda q, i, p: (q, 0, i))
    at_peer = pl.BlockSpec((block, sub), lambda q, i, p: (i, q * n_row + p[0]))
    packed = pl.BlockSpec((block, sub), lambda q, i, p: (i, q))
    kept = [pl.BlockSpec(memory_space=pl.ANY)] * len(before)
    out = jax.ShapeDtypeStruct(first_moment.shape, F32)
    return pl.pallas_call(
        moments_kernel,
        grid_spec=pltpu.PrefetchScalarGridSpec(
            num_scalar_prefetch=1,
            grid=(blocks, rows // block),
            in_specs=[packed_rot, at_peer, at_peer] + kept,
            out_specs=[at_peer, at_peer, packed],
        ),
        out_shape=[out, out, jax.ShapeDtypeStruct((rows, blocks * sub), BF16)],
        input_output_aliases={4: 0, 5: 1} if before else {},
        cost_estimate=pl.CostEstimate(
            flops=10 * rot.size, bytes_accessed=20 * rot.size, transcendentals=2 * rot.size
        ),
    )(peer.reshape(1), rot, first_moment, second_moment, *before)


def moments_sliced(peer, n_row, sub, rot, first_moment, second_moment, before):
    first_new, second_new = before if before else (first_moment, second_moment)
    directions = []
    for q in range(rot.shape[0]):
        start = (q * n_row + peer) * sub
        first, second, direction = moments(
            lax.dynamic_slice_in_dim(first_moment, start, sub, 1),
            lax.dynamic_slice_in_dim(second_moment, start, sub, 1),
            rot[q].astype(F32).T,
        )
        first_new = lax.dynamic_update_slice_in_dim(first_new, first, start, 1)
        second_new = lax.dynamic_update_slice_in_dim(second_new, second, start, 1)
        directions.append(direction)
    return first_new, second_new, jnp.concatenate(directions, axis=1)


def solution(mesh):
    n_row, n_col = mesh.shape["row"], mesh.shape["col"]
    n_a = 4
    n_b = n_col // n_a
    per_row = n_col // n_row

    def b_shift(x, db):
        perm = [(a * n_b + b, a * n_b + (b + db) % n_b) for a in range(n_a) for b in range(n_b)]
        return lax.ppermute(x, "col", perm)

    def a_shift(x, by):
        perm = [(a * n_b + b, (a + by) % n_a * n_b + b) for a in range(n_a) for b in range(n_b)]
        return lax.ppermute(x, "col", perm)

    def row_xor(x, k):
        return lax.ppermute(x, "row", [(r, r ^ k) for r in range(n_row)])

    def per_device(grad, basis_left, basis_right, first_moment, second_moment):
        last = {}

        def in_turn(link, x, move, depth):
            before = last.setdefault(link, [])
            if len(before) >= depth:
                x = tie(x, before[-depth])
            before.append(move(x))
            return before[-1]

        def across_b(x, k, depth=1):
            return in_turn("b", x, lambda y: b_shift(y, k), depth)

        def across_rows(x, k, depth=1):
            return row_xor(x, k) if k == 1 else in_turn("rows", x, lambda y: row_xor(y, k), depth)

        def half_sum(theirs, mine, depth):
            got = row_xor(theirs().astype(BF16), 1)
            mine = (mine() + got.astype(F32)).astype(BF16)
            last["half"] = mine
            k = 2
            while k < n_row:
                got = across_rows(mine, k, depth)
                mine = (mine.astype(F32) + got.astype(F32)).astype(BF16)
                k *= 2
            return mine, row_xor(mine, 1)

        r = lax.axis_index("row")
        c = lax.axis_index("col")
        a, b = c // n_b, c % n_b
        core = r % 2
        width = grad.shape[1]
        half = width // 2
        sub = width // n_row
        own_i = basis_left.shape[1]
        row_n = basis_right.shape[0]

        def n_at(s, h):
            return (a - s) % n_a * width + h * half

        def halves(x):
            return x[:, :half], x[:, half:]

        grad = jnp.concatenate(
            [lax.dynamic_slice_in_dim(grad, h * half, half, 1).T for h in (core, 1 - core)], axis=0
        )
        grad = lax.optimization_barrier(grad)
        below, above = a_shift(grad, 1), a_shift(grad, -1)
        grads = [grad, below, a_shift(below, 1), above]

        own_left = tie(basis_left, grad)
        lefts = [own_left] + [across_b(own_left, -k) for k in range(1, n_b)]

        right_after = tie(basis_right, grad)
        right_n = jnp.zeros((sub, n_row * row_n), BF16)
        for k in range(n_row):
            part = lax.dynamic_slice_in_dim(right_after, (r ^ k) * sub, sub, 1).T
            if k:
                part = across_rows(part, k, 2)
            right_n = lax.dynamic_update_slice_in_dim(right_n, part, (r ^ k) * row_n, 1)
        by_b = right_n.reshape(sub, n_a, n_b, width)

        def rows_of(which):
            return lax.dynamic_index_in_dim(by_b, which, 2, keepdims=False).reshape(sub, n_a * width)

        got = [rows_of(b)] + [across_b(rows_of((b + k) % n_b), k) for k in range(1, n_b)]
        stacked = jnp.stack(got, 0)
        right = [lax.dynamic_index_in_dim(stacked, (b - q) % n_b, 0, keepdims=False) for q in range(n_b)]
        right = jnp.concatenate(right, axis=0)

        near, far, last_b = (0, 1, 3), 2, n_b - 1
        turns = [(0, 0)] + [(k, s) for k in range(1, n_b) for s in near] + [(0, 1)]
        turns += [(k, far) for k in range(1, n_b)] + [(0, 3), (0, far)]
        rotated = [jnp.zeros((n_a * width, own_i), BF16) for _ in range(n_b)]
        for k, s in turns:
            if (k, s) == (1, 0):
                grads[1], grads[3], *lefts[1:] = tie((grads[1], grads[3], *lefts[1:]), right_n)
            if (k, s) == (1, 1):
                sent = tie(right, last["rows"][-1])
                below, above = a_shift(sent, 1), a_shift(sent, -1)
                rights = [right, below, a_shift(below, 1), above]
            if (k, s) == (1, far):
                grads[far] = tie(grads[far], last["rows"][-2])
            g = grads[s]
            g_mine, g_theirs = g[:half], g[half:]
            mine, theirs = half_sum(
                lambda: dot(g_theirs, lefts[k], (1, 0)), lambda: dot(g_mine, lefts[k], (1, 0)), 1
            )
            rotated[k] = lax.dynamic_update_slice_in_dim(rotated[k], mine, n_at(s, core), 0)
            rotated[k] = lax.dynamic_update_slice_in_dim(rotated[k], theirs, n_at(s, 1 - core), 0)
        left = jnp.concatenate(lefts, axis=1)

        rot_k = jnp.zeros((n_col, sub, own_i), BF16)
        right_k = jnp.zeros((n_col * sub, n_a * width), BF16)
        swapped = []
        for t in near + (far,):
            right_t = tie(rights[t], *swapped[-2:-1])
            rot = dot(right_t, rotated[0], (1, 0))
            for k in range(1, n_b):
                part = dot(right_t, rotated[k], (1, 0))
                swapped.append(across_b(part.astype(BF16), k))
                rot = rot + swapped[-1].astype(F32)
            rot = rot.astype(BF16)
            for q in range(n_b):
                block = (a - t) % n_a * n_b + q
                at = (block // per_row ^ r) * per_row + block % per_row
                rows = slice(q * sub, (q + 1) * sub)
                rot_k = lax.dynamic_update_index_in_dim(rot_k, rot[rows], at, 0)
                right_k = lax.dynamic_update_slice_in_dim(right_k, right_t[rows], at * sub, 0)

        step = moments_at if sub % 128 == 0 else moments_sliced
        rots = [rot_k[k * per_row : (k + 1) * per_row] for k in range(n_row)]
        rots[1:] = [across_rows(rots[k], k, 2) for k in range(1, n_row)]

        kept, by_rows = (), [[] for _ in range(n_b)]
        for k, rot in enumerate(rots):
            if k == n_row - 1:
                kept = tie(tuple(kept), by_rows[1][0])
            *kept, direction = step(r ^ k, n_row, sub, rot, first_moment, second_moment, tuple(kept))
            if k:
                direction = across_rows(direction, k, 2)
            by_rows[0].append(direction)
            for q in range(1, n_b):
                by_rows[q].append(across_b(direction, -q, 2))
        first_new, second_new = kept
        by_rows = [jnp.concatenate(ds, axis=1) for ds in by_rows]
        direction = jnp.concatenate(by_rows, axis=0)

        def back(s, parts):
            r_mine = lax.dynamic_slice_in_dim(right_k, n_at(s, core), half, 1)
            r_theirs = lax.dynamic_slice_in_dim(right_k, n_at(s, 1 - core), half, 1)
            u_mine = u_theirs = 0.0
            for i, (d, l) in enumerate(parts):
                if i:
                    d = tie(d, last["half"])
                w_mine, w_theirs = half_sum(
                    lambda: dot(d, r_theirs, (1, 0)), lambda: dot(d, r_mine, (1, 0)), 1
                )
                u_mine = u_mine + dot(l, w_mine, (1, 0))
                u_theirs = u_theirs + dot(l, w_theirs, (1, 0))
            return u_mine, u_theirs

        def joined(u):
            return jnp.concatenate([x.astype(BF16) for x in u], axis=1)

        whole = [(direction, left)]
        passed = halves(a_shift(joined(back(2, list(zip(by_rows, lefts)))), 1))
        behind = halves(a_shift(joined(back(1, whole)), -1))
        ahead = lax.optimization_barrier(back(3, whole))
        ahead = halves(a_shift(joined([u + x.astype(F32) for u, x in zip(ahead, passed)]), 1))
        own = lax.optimization_barrier(back(0, whole))
        u_mine, u_theirs = [
            (u + x.astype(F32) + y.astype(F32)).astype(BF16) for u, x, y in zip(own, behind, ahead)
        ]
        update = jnp.where(
            core == 0,
            jnp.concatenate([u_mine, u_theirs], axis=1),
            jnp.concatenate([u_theirs, u_mine], axis=1),
        )
        return update, first_new, second_new

    in_specs = (P("row", "col"), P("row", "col"), P("row", "col"), P("col", "row"), P("col", "row"))
    out_specs = (P("row", "col"), P("col", "row"), P("col", "row"))
    return jax.shard_map(per_device, mesh=mesh, in_specs=in_specs, out_specs=out_specs, check_vma=False)
```

```python
import functools

import jax
import jax.numpy as jnp
from jax import lax
from jax.experimental import pallas as pl
from jax.experimental.pallas import tpu as pltpu
from jax.sharding import PartitionSpec as P

BF16 = jnp.bfloat16
F32 = jnp.float32


def dot(a, b, contract):
    return lax.dot_general(a, b, ((contract[:1], contract[1:]), ((), ())), preferred_element_type=F32)


def tie(x, *earlier):
    return lax.optimization_barrier((x, *earlier))[0]


def product_kernel(n_pairs, *refs):
    out = refs[-1]
    total = None
    for x, y in zip(refs[:n_pairs], refs[n_pairs : 2 * n_pairs]):
        term = jnp.dot(x[...], y[...], preferred_element_type=F32)
        total = term if total is None else total + term
    for more in refs[2 * n_pairs : -1]:
        total = total + more[...].astype(F32)
    out[...] = total.astype(out.dtype)


def product(pairs, kind, more=(), by_rows=True):
    rows, columns = pairs[0][0].shape[0], pairs[0][1].shape[1]
    if by_rows:
        block = min(rows, 512)
        grid, out = rows // block, pl.BlockSpec((block, columns), lambda i: (i, 0))
        xs = [pl.BlockSpec((block, x.shape[1]), lambda i: (i, 0)) for x, _ in pairs]
        ys = [pl.BlockSpec(y.shape, lambda i: (0, 0)) for _, y in pairs]
    else:
        block = min(columns, 256)
        grid, out = columns // block, pl.BlockSpec((rows, block), lambda i: (0, i))
        xs = [pl.BlockSpec(x.shape, lambda i: (0, 0)) for x, _ in pairs]
        ys = [pl.BlockSpec((y.shape[0], block), lambda i: (0, i)) for _, y in pairs]
    return pl.pallas_call(
        functools.partial(product_kernel, len(pairs)),
        grid=(grid,),
        in_specs=xs + ys + [out] * len(more),
        out_specs=out,
        out_shape=jax.ShapeDtypeStruct((rows, columns), kind),
        cost_estimate=pl.CostEstimate(flops=512 * rows * columns, bytes_accessed=0, transcendentals=0),
        compiler_params=pltpu.CompilerParams(vmem_limit_bytes=16 * 2**20),
    )(*[x for x, _ in pairs], *[y for _, y in pairs], *more)


def moments(first, second, rot):
    first = 0.9 * first + 0.1 * rot
    second = 0.95 * second + 0.05 * rot * rot
    return first, second, (first / (jnp.sqrt(second) + 1e-08)).astype(BF16)


def moments_kernel(peer_ref, rot_ref, first_ref, second_ref, *refs):
    first_new, second_new, direction = refs[-3:]
    first_new[...], second_new[...], direction[...] = moments(
        first_ref[...], second_ref[...], rot_ref[0].astype(F32).T
    )


def moments_at(peer, n_row, sub, rot, first_moment, second_moment, before):
    blocks, _, rows = rot.shape
    block = min(rows, 512)
    packed_rot = pl.BlockSpec((1, sub, block), lambda q, i, p: (q, 0, i))
    at_peer = pl.BlockSpec((block, sub), lambda q, i, p: (i, q * n_row + p[0]))
    packed = pl.BlockSpec((block, sub), lambda q, i, p: (i, q))
    kept = [pl.BlockSpec(memory_space=pl.ANY)] * len(before)
    out = jax.ShapeDtypeStruct(first_moment.shape, F32)
    return pl.pallas_call(
        moments_kernel,
        grid_spec=pltpu.PrefetchScalarGridSpec(
            num_scalar_prefetch=1,
            grid=(blocks, rows // block),
            in_specs=[packed_rot, at_peer, at_peer] + kept,
            out_specs=[at_peer, at_peer, packed],
        ),
        out_shape=[out, out, jax.ShapeDtypeStruct((rows, blocks * sub), BF16)],
        input_output_aliases={4: 0, 5: 1} if before else {},
        compiler_params=pltpu.CompilerParams(vmem_limit_bytes=16 * 2**20),
        cost_estimate=pl.CostEstimate(
            flops=10 * rot.size, bytes_accessed=20 * rot.size, transcendentals=2 * rot.size
        ),
    )(peer.reshape(1), rot, first_moment, second_moment, *before)


def moments_sliced(peer, n_row, sub, rot, first_moment, second_moment, before):
    first_new, second_new = before if before else (first_moment, second_moment)
    directions = []
    for q in range(rot.shape[0]):
        start = (q * n_row + peer) * sub
        first, second, direction = moments(
            lax.dynamic_slice_in_dim(first_moment, start, sub, 1),
            lax.dynamic_slice_in_dim(second_moment, start, sub, 1),
            rot[q].astype(F32).T,
        )
        first_new = lax.dynamic_update_slice_in_dim(first_new, first, start, 1)
        second_new = lax.dynamic_update_slice_in_dim(second_new, second, start, 1)
        directions.append(direction)
    return first_new, second_new, jnp.concatenate(directions, axis=1)


def solution(mesh):
    n_row, n_col = mesh.shape["row"], mesh.shape["col"]
    n_a = 4
    n_b = n_col // n_a
    per_row = n_col // n_row

    def b_shift(x, db):
        perm = [(a * n_b + b, a * n_b + (b + db) % n_b) for a in range(n_a) for b in range(n_b)]
        return lax.ppermute(x, "col", perm)

    def a_shift(x, by):
        perm = [(a * n_b + b, (a + by) % n_a * n_b + b) for a in range(n_a) for b in range(n_b)]
        return lax.ppermute(x, "col", perm)

    def row_xor(x, k):
        return lax.ppermute(x, "row", [(r, r ^ k) for r in range(n_row)])

    def per_device(grad, basis_left, basis_right, first_moment, second_moment):
        last = {}

        def in_turn(link, x, move, depth):
            before = last.setdefault(link, [])
            if len(before) >= depth:
                x = tie(x, before[-depth])
            before.append(move(x))
            return before[-1]

        def across_b(x, k, depth=1):
            return in_turn("b", x, lambda y: b_shift(y, k), depth)

        def across_rows(x, k, depth=1):
            return row_xor(x, k) if k == 1 else in_turn("rows", x, lambda y: row_xor(y, k), depth)

        def half_sum(theirs, mine, depth):
            mine = mine(row_xor(theirs(), 1))
            last["half"] = mine
            k = 2
            while k < n_row:
                got = across_rows(mine, k, depth)
                mine = (mine.astype(F32) + got.astype(F32)).astype(BF16)
                k *= 2
            return mine, row_xor(mine, 1)

        r = lax.axis_index("row")
        c = lax.axis_index("col")
        a, b = c // n_b, c % n_b
        core = r % 2
        width = grad.shape[1]
        half = width // 2
        sub = width // n_row
        own_i = basis_left.shape[1]
        row_n = basis_right.shape[0]

        def n_at(s, h):
            return (a - s) % n_a * width + h * half

        def halves(x):
            return x[:, :half], x[:, half:]

        grad = jnp.concatenate(
            [lax.dynamic_slice_in_dim(grad, h * half, half, 1).T for h in (core, 1 - core)], axis=0
        )
        grad = lax.optimization_barrier(grad)
        below, above = a_shift(grad, 1), a_shift(grad, -1)
        grads = [grad, below, a_shift(below, 1), above]

        own_left = tie(basis_left, grad)
        lefts = [own_left] + [across_b(own_left, -k) for k in range(1, n_b)]

        right_after = tie(basis_right, grad)
        right_n = jnp.zeros((sub, n_row * row_n), BF16)
        for k in range(n_row):
            part = lax.dynamic_slice_in_dim(right_after, (r ^ k) * sub, sub, 1).T
            if k:
                part = across_rows(part, k, 2)
            right_n = lax.dynamic_update_slice_in_dim(right_n, part, (r ^ k) * row_n, 1)
        by_b = right_n.reshape(sub, n_a, n_b, width)

        def rows_of(which):
            return lax.dynamic_index_in_dim(by_b, which, 2, keepdims=False).reshape(sub, n_a * width)

        got = [rows_of(b)] + [across_b(rows_of((b + k) % n_b), k) for k in range(1, n_b)]
        stacked = jnp.stack(got, 0)
        right = [lax.dynamic_index_in_dim(stacked, (b - q) % n_b, 0, keepdims=False) for q in range(n_b)]
        right = jnp.concatenate(right, axis=0)

        near, far, last_b = (0, 1, 3), 2, n_b - 1
        turns = [(0, 0)] + [(k, s) for k in range(1, n_b) for s in near] + [(0, 1)]
        turns += [(k, far) for k in range(1, n_b)] + [(0, 3), (0, far)]
        rotated = [jnp.zeros((n_a * width, own_i), BF16) for _ in range(n_b)]
        for k, s in turns:
            if (k, s) == (1, 0):
                grads[1], grads[3], *lefts[1:] = tie((grads[1], grads[3], *lefts[1:]), right_n)
                sent = tie(right, grads[1], grads[3])
                below, above = a_shift(sent, 1), a_shift(sent, -1)
                rights = [right, below, a_shift(below, 1), above]
            if (k, s) == (1, 1):
                grads[1] = tie(grads[1], right)
            if (k, s) == (1, far):
                grads[far] = tie(grads[far], last["rows"][-2])
            g = tie(grads[s], rights[1]) if (k, s) == turns[-1] else grads[s]
            g_mine, g_theirs = g[:half], g[half:]
            mine, theirs = half_sum(
                lambda: product([(g_theirs, lefts[k])], BF16, by_rows=False),
                lambda got: product([(g_mine, lefts[k])], BF16, (got,), by_rows=False),
                1,
            )
            rotated[k] = lax.dynamic_update_slice_in_dim(rotated[k], mine, n_at(s, core), 0)
            rotated[k] = lax.dynamic_update_slice_in_dim(rotated[k], theirs, n_at(s, 1 - core), 0)
        rot_k = jnp.zeros((n_col, sub, own_i), BF16)
        right_k = jnp.zeros((n_col * sub, n_a * width), BF16)
        swapped = []
        for t in near + (far,):
            right_t = tie(rights[t], *swapped[-2:-1])
            rot = dot(right_t, rotated[0], (1, 0))
            for k in range(1, n_b):
                part = dot(right_t, rotated[k], (1, 0))
                swapped.append(across_b(part.astype(BF16), k))
                rot = rot + swapped[-1].astype(F32)
            rot = rot.astype(BF16)
            for q in range(n_b):
                block = (a - t) % n_a * n_b + q
                at = (block // per_row ^ r) * per_row + block % per_row
                rows = slice(q * sub, (q + 1) * sub)
                rot_k = lax.dynamic_update_index_in_dim(rot_k, rot[rows], at, 0)
                right_k = lax.dynamic_update_slice_in_dim(right_k, right_t[rows], at * sub, 0)

        step = moments_at if sub % 128 == 0 else moments_sliced
        rots = [rot_k[k * per_row : (k + 1) * per_row] for k in range(n_row)]
        rots[1:] = [across_rows(rots[k], k, 2) for k in range(1, n_row)]

        kept, by_rows = (), [[] for _ in range(n_b)]
        for k, rot in enumerate(rots):
            if k == n_row - 1:
                kept = tie(tuple(kept), by_rows[1][0])
            *kept, direction = step(r ^ k, n_row, sub, rot, first_moment, second_moment, tuple(kept))
            if k:
                direction = across_rows(direction, k)
            by_rows[0].append(direction)
            for q in range(1, n_b):
                by_rows[q].append(across_b(direction, -q))
        first_new, second_new = kept
        by_rows = [jnp.concatenate(ds, axis=1) for ds in by_rows]
        direction = jnp.concatenate(by_rows, axis=0)

        def back(s, parts, kind):
            r_mine = lax.dynamic_slice_in_dim(right_k, n_at(s, core), half, 1)
            r_theirs = lax.dynamic_slice_in_dim(right_k, n_at(s, 1 - core), half, 1)
            w_mine, w_theirs = [], []
            for i, d in enumerate(parts):
                d_mine = d
                if i:
                    d, d_mine = tie(d, last["half"]), tie(d, last["rows"][-1])
                mine, theirs = half_sum(
                    lambda: dot(d, r_theirs, (1, 0)).astype(BF16),
                    lambda got: (dot(d_mine, r_mine, (1, 0)) + got.astype(F32)).astype(BF16),
                    1,
                )
                w_mine.append(mine)
                w_theirs.append(theirs)
            if len(parts) < n_b:
                w_mine, w_theirs = [
                    [w[0][k * own_i : (k + 1) * own_i] for k in range(n_b)] for w in (w_mine, w_theirs)
                ]
            return [product(list(zip(lefts, w)), kind) for w in (w_mine, w_theirs)]

        def joined(u):
            return jnp.concatenate(u, axis=1)

        whole = [direction]
        passed = halves(a_shift(joined(back(2, by_rows, BF16)), 1))
        behind = halves(a_shift(joined(back(1, whole, BF16)), -1))
        ahead = [(u + x.astype(F32)).astype(BF16) for u, x in zip(back(3, whole, F32), passed)]
        ahead = halves(a_shift(joined(ahead), 1))
        own = back(0, whole, F32)
        u_mine, u_theirs = [
            (u + x.astype(F32) + y.astype(F32)).astype(BF16) for u, x, y in zip(own, behind, ahead)
        ]
        update = jnp.where(
            core == 0,
            jnp.concatenate([u_mine, u_theirs], axis=1),
            jnp.concatenate([u_theirs, u_mine], axis=1),
        )
        return update, first_new, second_new

    in_specs = (P("row", "col"), P("row", "col"), P("row", "col"), P("col", "row"), P("col", "row"))
    out_specs = (P("row", "col"), P("col", "row"), P("col", "row"))
    return jax.shard_map(per_device, mesh=mesh, in_specs=in_specs, out_specs=out_specs, check_vma=False)
```

```python
import functools

import jax
import jax.numpy as jnp
from jax import lax
from jax.experimental import pallas as pl
from jax.experimental.pallas import tpu as pltpu
from jax.sharding import PartitionSpec as P

BF16 = jnp.bfloat16
F32 = jnp.float32


def dot(a, b, contract):
    return lax.dot_general(a, b, ((contract[:1], contract[1:]), ((), ())), preferred_element_type=F32)


def tie(x, *earlier):
    return lax.optimization_barrier((x, *earlier))[0]


def product_kernel(n_pairs, *refs):
    out = refs[-1]
    total = None
    for x, y in zip(refs[:n_pairs], refs[n_pairs : 2 * n_pairs]):
        term = jnp.dot(x[...], y[...], preferred_element_type=F32)
        total = term if total is None else total + term
    for more in refs[2 * n_pairs : -1]:
        total = total + more[...].astype(F32)
    out[...] = total.astype(out.dtype)


def product(pairs, kind, more=(), by_rows=True):
    rows, columns = pairs[0][0].shape[0], pairs[0][1].shape[1]
    if by_rows:
        block = min(rows, 512)
        grid, out = rows // block, pl.BlockSpec((block, columns), lambda i: (i, 0))
        xs = [pl.BlockSpec((block, x.shape[1]), lambda i: (i, 0)) for x, _ in pairs]
        ys = [pl.BlockSpec(y.shape, lambda i: (0, 0)) for _, y in pairs]
    else:
        block = min(columns, 256)
        grid, out = columns // block, pl.BlockSpec((rows, block), lambda i: (0, i))
        xs = [pl.BlockSpec(x.shape, lambda i: (0, 0)) for x, _ in pairs]
        ys = [pl.BlockSpec((y.shape[0], block), lambda i: (0, i)) for _, y in pairs]
    return pl.pallas_call(
        functools.partial(product_kernel, len(pairs)),
        grid=(grid,),
        in_specs=xs + ys + [out] * len(more),
        out_specs=out,
        out_shape=jax.ShapeDtypeStruct((rows, columns), kind),
        cost_estimate=pl.CostEstimate(flops=512 * rows * columns, bytes_accessed=0, transcendentals=0),
        compiler_params=pltpu.CompilerParams(vmem_limit_bytes=16 * 2**20),
    )(*[x for x, _ in pairs], *[y for _, y in pairs], *more)


def moments(first, second, rot):
    first = 0.9 * first + 0.1 * rot
    second = 0.95 * second + 0.05 * rot * rot
    return first, second, (first / (jnp.sqrt(second) + 1e-08)).astype(BF16)


def moments_kernel(peer_ref, rot_ref, first_ref, second_ref, *refs):
    first_new, second_new, direction = refs[-3:]
    first_new[...], second_new[...], direction[...] = moments(
        first_ref[...], second_ref[...], rot_ref[0].astype(F32).T
    )


def moments_at(peer, n_row, sub, rot, first_moment, second_moment, before):
    blocks, _, rows = rot.shape
    block = min(rows, 512)
    packed_rot = pl.BlockSpec((1, sub, block), lambda q, i, p: (q, 0, i))
    at_peer = pl.BlockSpec((block, sub), lambda q, i, p: (i, q * n_row + p[0]))
    packed = pl.BlockSpec((block, sub), lambda q, i, p: (i, q))
    kept = [pl.BlockSpec(memory_space=pl.ANY)] * len(before)
    out = jax.ShapeDtypeStruct(first_moment.shape, F32)
    return pl.pallas_call(
        moments_kernel,
        grid_spec=pltpu.PrefetchScalarGridSpec(
            num_scalar_prefetch=1,
            grid=(blocks, rows // block),
            in_specs=[packed_rot, at_peer, at_peer] + kept,
            out_specs=[at_peer, at_peer, packed],
        ),
        out_shape=[out, out, jax.ShapeDtypeStruct((rows, blocks * sub), BF16)],
        input_output_aliases={4: 0, 5: 1} if before else {},
        compiler_params=pltpu.CompilerParams(vmem_limit_bytes=16 * 2**20),
        cost_estimate=pl.CostEstimate(
            flops=10 * rot.size, bytes_accessed=20 * rot.size, transcendentals=2 * rot.size
        ),
    )(peer.reshape(1), rot, first_moment, second_moment, *before)


def moments_sliced(peer, n_row, sub, rot, first_moment, second_moment, before):
    first_new, second_new = before if before else (first_moment, second_moment)
    directions = []
    for q in range(rot.shape[0]):
        start = (q * n_row + peer) * sub
        first, second, direction = moments(
            lax.dynamic_slice_in_dim(first_moment, start, sub, 1),
            lax.dynamic_slice_in_dim(second_moment, start, sub, 1),
            rot[q].astype(F32).T,
        )
        first_new = lax.dynamic_update_slice_in_dim(first_new, first, start, 1)
        second_new = lax.dynamic_update_slice_in_dim(second_new, second, start, 1)
        directions.append(direction)
    return first_new, second_new, jnp.concatenate(directions, axis=1)


def solution(mesh):
    n_row, n_col = mesh.shape["row"], mesh.shape["col"]
    n_a = 4
    n_b = n_col // n_a
    per_row = n_col // n_row

    def b_shift(x, db):
        perm = [(a * n_b + b, a * n_b + (b + db) % n_b) for a in range(n_a) for b in range(n_b)]
        return lax.ppermute(x, "col", perm)

    def a_shift(x, by):
        perm = [(a * n_b + b, (a + by) % n_a * n_b + b) for a in range(n_a) for b in range(n_b)]
        return lax.ppermute(x, "col", perm)

    def row_xor(x, k):
        return lax.ppermute(x, "row", [(r, r ^ k) for r in range(n_row)])

    def per_device(grad, basis_left, basis_right, first_moment, second_moment):
        last = {}

        def in_turn(link, x, move, depth):
            before = last.setdefault(link, [])
            if len(before) >= depth:
                x = tie(x, before[-depth])
            before.append(move(x))
            return before[-1]

        def across_b(x, k, depth=1):
            return in_turn("b", x, lambda y: b_shift(y, k), depth)

        def across_rows(x, k, depth=1):
            return row_xor(x, k) if k == 1 else in_turn("rows", x, lambda y: row_xor(y, k), depth)

        def half_sum(theirs, mine, depth):
            mine = (mine.astype(F32) + row_xor(theirs.astype(BF16), 1).astype(F32)).astype(BF16)
            last["half"] = mine
            k = 2
            while k < n_row:
                got = across_rows(mine, k, depth)
                mine = (mine.astype(F32) + got.astype(F32)).astype(BF16)
                k *= 2
            return mine, row_xor(mine, 1)

        r = lax.axis_index("row")
        c = lax.axis_index("col")
        a, b = c // n_b, c % n_b
        core = r % 2
        width = grad.shape[1]
        half = width // 2
        sub = width // n_row
        own_i = basis_left.shape[1]
        row_n = basis_right.shape[0]

        def n_at(s, h):
            return (a - s) % n_a * width + h * half

        grad = jnp.concatenate(
            [lax.dynamic_slice_in_dim(grad, h * half, half, 1).T for h in (core, 1 - core)], axis=0
        )
        grad = lax.optimization_barrier(grad)
        below, above = a_shift(grad, 1), a_shift(grad, -1)
        grads = [grad, below, a_shift(below, 1), above]

        own_left = tie(basis_left, grad)
        lefts = [own_left] + [across_b(own_left, -k) for k in range(1, n_b)]

        right_after = tie(basis_right, grad)
        right_n = jnp.zeros((sub, n_row * row_n), BF16)
        for k in range(n_row):
            part = lax.dynamic_slice_in_dim(right_after, (r ^ k) * sub, sub, 1).T
            if k:
                part = across_rows(part, k, 2)
            right_n = lax.dynamic_update_slice_in_dim(right_n, part, (r ^ k) * row_n, 1)
        by_b = right_n.reshape(sub, n_a, n_b, width)

        def rows_of(which):
            return lax.dynamic_index_in_dim(by_b, which, 2, keepdims=False).reshape(sub, n_a * width)

        got = [rows_of(b)] + [across_b(rows_of((b + k) % n_b), k, 2) for k in range(1, n_b)]
        stacked = jnp.stack(got, 0)
        right = [lax.dynamic_index_in_dim(stacked, (b - q) % n_b, 0, keepdims=False) for q in range(n_b)]
        right = jnp.concatenate(right, axis=0)

        near, far, last_b = (0, 1, 3), 2, n_b - 1
        turns = [(0, 0)] + [(k, s) for k in range(1, n_b) for s in near] + [(0, 1)]
        turns += [(k, far) for k in range(1, n_b)] + [(0, 3), (0, far)]
        rotated = [jnp.zeros((n_a * width, own_i), BF16) for _ in range(n_b)]
        for k, s in turns:
            if (k, s) == (1, 0):
                grads[1], grads[3], *lefts[1:] = tie((grads[1], grads[3], *lefts[1:]), right_n)
                sent = tie(right, grads[1], grads[3])
                below, above = a_shift(sent, 1), a_shift(sent, -1)
                rights = [right, below, a_shift(below, 1), above]
            if (k, s) == (1, 1):
                grads[1] = tie(grads[1], right)
            if (k, s) == (1, far):
                grads[far] = tie(grads[far], last["rows"][-2])
            g = tie(grads[s], rights[1], rights[3]) if (k, s) == turns[-1] else grads[s]
            term = product([(g, lefts[k])], BF16, by_rows=False)
            mine, theirs = half_sum(term[half:], term[:half], 1)
            rotated[k] = lax.dynamic_update_slice_in_dim(rotated[k], mine, n_at(s, core), 0)
            rotated[k] = lax.dynamic_update_slice_in_dim(rotated[k], theirs, n_at(s, 1 - core), 0)
        rot_k = jnp.zeros((n_col, sub, own_i), BF16)
        right_k = jnp.zeros((n_col * sub, n_a * width), BF16)
        swapped = []
        for t in near + (far,):
            right_t = tie(rights[t], *swapped[-2:-1])
            rot = dot(right_t, rotated[0], (1, 0))
            for k in range(1, n_b):
                part = dot(right_t, rotated[k], (1, 0))
                swapped.append(across_b(part.astype(BF16), k))
                rot = rot + swapped[-1].astype(F32)
            rot = rot.astype(BF16)
            for q in range(n_b):
                block = (a - t) % n_a * n_b + q
                at = (block // per_row ^ r) * per_row + block % per_row
                rows = slice(q * sub, (q + 1) * sub)
                rot_k = lax.dynamic_update_index_in_dim(rot_k, rot[rows], at, 0)
                right_k = lax.dynamic_update_slice_in_dim(right_k, right_t[rows], at * sub, 0)

        step = moments_at if sub % 128 == 0 else moments_sliced
        rots = [rot_k[k * per_row : (k + 1) * per_row] for k in range(n_row)]
        rots[1:] = [across_rows(rots[k], k, 2) for k in range(1, n_row)]

        kept, by_rows, held = (), [[] for _ in range(n_b)], []
        for k, rot in enumerate(rots):
            *kept, direction = step(r ^ k, n_row, sub, rot, first_moment, second_moment, tuple(kept))
            if k:
                direction = across_rows(direction, k)
            held.append(direction)
            if k:
                direction = jnp.concatenate(held, axis=1)
                held = []
                by_rows[0].append(direction)
                for q in range(1, n_b):
                    by_rows[q].append(across_b(direction, -q))
        first_new, second_new = kept
        by_rows = [jnp.concatenate(ds, axis=1) for ds in by_rows]
        direction = jnp.concatenate(by_rows, axis=0)

        def back(s, parts, kind, more=()):
            r_mine = lax.dynamic_slice_in_dim(right_k, n_at(s, core), half, 1)
            r_theirs = lax.dynamic_slice_in_dim(right_k, n_at(s, 1 - core), half, 1)
            ws = []
            for i, d in enumerate(parts):
                d_mine = d
                if i:
                    d, d_mine = tie(d, last["half"]), tie(d, last["rows"][-1])
                ws.append(jnp.concatenate(half_sum(dot(d, r_theirs, (1, 0)), dot(d_mine, r_mine, (1, 0)), 1), axis=1))
            if len(parts) < n_b:
                ws = [ws[0][k * own_i : (k + 1) * own_i] for k in range(n_b)]
            return product(list(zip(lefts, ws)), kind, more)

        whole = [direction]
        passed = a_shift(back(2, by_rows, BF16), 1)
        behind = a_shift(back(1, whole, BF16), -1)
        ahead = a_shift((back(3, whole, F32) + passed.astype(F32)).astype(BF16), 1)
        update = back(0, whole, F32) + behind.astype(F32) + ahead.astype(F32)
        u_mine, u_theirs = update[:, :half].astype(BF16), update[:, half:].astype(BF16)
        update = jnp.where(
            core == 0,
            jnp.concatenate([u_mine, u_theirs], axis=1),
            jnp.concatenate([u_theirs, u_mine], axis=1),
        )
        return update, first_new, second_new

    in_specs = (P("row", "col"), P("row", "col"), P("row", "col"), P("col", "row"), P("col", "row"))
    out_specs = (P("row", "col"), P("col", "row"), P("col", "row"))
    return jax.shard_map(per_device, mesh=mesh, in_specs=in_specs, out_specs=out_specs, check_vma=False)
```

```python
import functools

import jax
import jax.numpy as jnp
from jax import lax
from jax.experimental import pallas as pl
from jax.experimental.pallas import tpu as pltpu
from jax.sharding import PartitionSpec as P

BF16 = jnp.bfloat16
F32 = jnp.float32


def dot(a, b, contract):
    return lax.dot_general(a, b, ((contract[:1], contract[1:]), ((), ())), preferred_element_type=F32)


def tie(x, *earlier):
    return lax.optimization_barrier((x, *earlier))[0]


def product_kernel(n_pairs, *refs):
    out = refs[-1]
    total = None
    for x, y in zip(refs[:n_pairs], refs[n_pairs : 2 * n_pairs]):
        term = jnp.dot(x[...], y[...], preferred_element_type=F32)
        total = term if total is None else total + term
    for more in refs[2 * n_pairs : -1]:
        total = total + more[...].astype(F32)
    out[...] = total.astype(out.dtype)


def product(pairs, kind, more=(), by_rows=True):
    rows, columns = pairs[0][0].shape[0], pairs[0][1].shape[1]
    if by_rows:
        block = min(rows, 512)
        grid, out = rows // block, pl.BlockSpec((block, columns), lambda i: (i, 0))
        xs = [pl.BlockSpec((block, x.shape[1]), lambda i: (i, 0)) for x, _ in pairs]
        ys = [pl.BlockSpec(y.shape, lambda i: (0, 0)) for _, y in pairs]
    else:
        block = min(columns, 256)
        grid, out = columns // block, pl.BlockSpec((rows, block), lambda i: (0, i))
        xs = [pl.BlockSpec(x.shape, lambda i: (0, 0)) for x, _ in pairs]
        ys = [pl.BlockSpec((y.shape[0], block), lambda i: (0, i)) for _, y in pairs]
    return pl.pallas_call(
        functools.partial(product_kernel, len(pairs)),
        grid=(grid,),
        in_specs=xs + ys + [out] * len(more),
        out_specs=out,
        out_shape=jax.ShapeDtypeStruct((rows, columns), kind),
        cost_estimate=pl.CostEstimate(flops=512 * rows * columns, bytes_accessed=0, transcendentals=0),
        compiler_params=pltpu.CompilerParams(vmem_limit_bytes=16 * 2**20),
    )(*[x for x, _ in pairs], *[y for _, y in pairs], *more)


def moments(first, second, rot):
    first = 0.9 * first + 0.1 * rot
    second = 0.95 * second + 0.05 * rot * rot
    return first, second, (first / (jnp.sqrt(second) + 1e-08)).astype(BF16)


def moments_kernel(peer_ref, rot_ref, first_ref, second_ref, *refs):
    first_new, second_new, direction = refs[-3:]
    first_new[...], second_new[...], direction[...] = moments(
        first_ref[...], second_ref[...], rot_ref[0].astype(F32).T
    )


def moments_at(peer, n_row, sub, rot, first_moment, second_moment, before):
    blocks, _, rows = rot.shape
    block = min(rows, 512)
    packed_rot = pl.BlockSpec((1, sub, block), lambda q, i, p: (q, 0, i))
    at_peer = pl.BlockSpec((block, sub), lambda q, i, p: (i, q * n_row + p[0]))
    packed = pl.BlockSpec((block, sub), lambda q, i, p: (i, q))
    kept = [pl.BlockSpec(memory_space=pl.ANY)] * len(before)
    out = jax.ShapeDtypeStruct(first_moment.shape, F32)
    return pl.pallas_call(
        moments_kernel,
        grid_spec=pltpu.PrefetchScalarGridSpec(
            num_scalar_prefetch=1,
            grid=(blocks, rows // block),
            in_specs=[packed_rot, at_peer, at_peer] + kept,
            out_specs=[at_peer, at_peer, packed],
        ),
        out_shape=[out, out, jax.ShapeDtypeStruct((rows, blocks * sub), BF16)],
        input_output_aliases={4: 0, 5: 1} if before else {},
        compiler_params=pltpu.CompilerParams(vmem_limit_bytes=16 * 2**20),
        cost_estimate=pl.CostEstimate(
            flops=10 * rot.size, bytes_accessed=20 * rot.size, transcendentals=2 * rot.size
        ),
    )(peer.reshape(1), rot, first_moment, second_moment, *before)


def moments_sliced(peer, n_row, sub, rot, first_moment, second_moment, before):
    first_new, second_new = before if before else (first_moment, second_moment)
    directions = []
    for q in range(rot.shape[0]):
        start = (q * n_row + peer) * sub
        first, second, direction = moments(
            lax.dynamic_slice_in_dim(first_moment, start, sub, 1),
            lax.dynamic_slice_in_dim(second_moment, start, sub, 1),
            rot[q].astype(F32).T,
        )
        first_new = lax.dynamic_update_slice_in_dim(first_new, first, start, 1)
        second_new = lax.dynamic_update_slice_in_dim(second_new, second, start, 1)
        directions.append(direction)
    return first_new, second_new, jnp.concatenate(directions, axis=1)


def solution(mesh):
    n_row, n_col = mesh.shape["row"], mesh.shape["col"]
    n_a = 4
    n_b = n_col // n_a
    per_row = n_col // n_row

    def b_shift(x, db):
        perm = [(a * n_b + b, a * n_b + (b + db) % n_b) for a in range(n_a) for b in range(n_b)]
        return lax.ppermute(x, "col", perm)

    def a_shift(x, by):
        perm = [(a * n_b + b, (a + by) % n_a * n_b + b) for a in range(n_a) for b in range(n_b)]
        return lax.ppermute(x, "col", perm)

    def row_xor(x, k):
        return lax.ppermute(x, "row", [(r, r ^ k) for r in range(n_row)])

    def per_device(grad, basis_left, basis_right, first_moment, second_moment):
        last = {}

        def in_turn(link, x, move, depth):
            before = last.setdefault(link, [])
            if len(before) >= depth:
                x = tie(x, before[-depth])
            before.append(move(x))
            return before[-1]

        def across_b(x, k, depth=1):
            return in_turn("b", x, lambda y: b_shift(y, k), depth)

        def across_rows(x, k, depth=1):
            return row_xor(x, k) if k == 1 else in_turn("rows", x, lambda y: row_xor(y, k), depth)

        def half_sum(theirs, mine, depth):
            mine = (mine.astype(F32) + row_xor(theirs.astype(BF16), 1).astype(F32)).astype(BF16)
            last["half"] = mine
            k = 2
            while k < n_row:
                got = across_rows(mine, k, depth)
                mine = (mine.astype(F32) + got.astype(F32)).astype(BF16)
                k *= 2
            return mine, row_xor(mine, 1)

        r = lax.axis_index("row")
        c = lax.axis_index("col")
        a, b = c // n_b, c % n_b
        core = r % 2
        width = grad.shape[1]
        half = width // 2
        sub = width // n_row
        own_i = basis_left.shape[1]
        row_n = basis_right.shape[0]

        def n_at(s, h):
            return (a - s) % n_a * width + h * half

        grad = jnp.concatenate(
            [lax.dynamic_slice_in_dim(grad, h * half, half, 1).T for h in (core, 1 - core)], axis=0
        )
        grad = lax.optimization_barrier(grad)
        below, above = a_shift(grad, 1), a_shift(grad, -1)
        grads = [grad, below, a_shift(below, 1), above]

        own_left = tie(basis_left, grad)
        lefts = [own_left] + [across_b(own_left, -k) for k in range(1, n_b)]

        right_after = tie(basis_right, grad)
        right_n = jnp.zeros((sub, n_row * row_n), BF16)
        for k in range(n_row):
            part = lax.dynamic_slice_in_dim(right_after, (r ^ k) * sub, sub, 1).T
            if k:
                part = across_rows(part, k, 2)
            right_n = lax.dynamic_update_slice_in_dim(right_n, part, (r ^ k) * row_n, 1)
        by_b = right_n.reshape(sub, n_a, n_b, width)

        def rows_of(which):
            return lax.dynamic_index_in_dim(by_b, which, 2, keepdims=False).reshape(sub, n_a * width)

        got = [rows_of(b)] + [across_b(rows_of((b + k) % n_b), k, 2) for k in range(1, n_b)]
        stacked = jnp.stack(got, 0)
        right = [lax.dynamic_index_in_dim(stacked, (b - q) % n_b, 0, keepdims=False) for q in range(n_b)]
        right = jnp.concatenate(right, axis=0)

        near, far, last_b = (0, 1, 3), 2, n_b - 1
        turns = [(0, 0)] + [(k, s) for k in range(1, n_b) for s in near] + [(0, 1)]
        turns += [(k, far) for k in range(1, n_b)] + [(0, 3), (0, far)]
        rotated = [jnp.zeros((n_a * width, own_i), BF16) for _ in range(n_b)]
        for k, s in turns:
            if (k, s) == (1, 0):
                grads[1], grads[3], *lefts[1:] = tie((grads[1], grads[3], *lefts[1:]), right_n)
                sent = tie(right, grads[1], grads[3])
                below, above = a_shift(sent, 1), a_shift(sent, -1)
                rights = [right, below, a_shift(below, 1), above]
            if (k, s) == (1, 1):
                grads[1] = tie(grads[1], right)
            if (k, s) == (1, far):
                grads[far] = tie(grads[far], last["rows"][-2])
            g = tie(grads[s], rights[1], rights[3]) if (k, s) == (0, 3) else grads[s]
            term = product([(g, lefts[k])], BF16, by_rows=False)
            mine, theirs = half_sum(term[half:], term[:half], 1)
            rotated[k] = lax.dynamic_update_slice_in_dim(rotated[k], mine, n_at(s, core), 0)
            rotated[k] = lax.dynamic_update_slice_in_dim(rotated[k], theirs, n_at(s, 1 - core), 0)
        rot_k = jnp.zeros((n_col, sub, own_i), BF16)
        right_k = jnp.zeros((n_col * sub, n_a * width), BF16)
        swapped = []
        for t in near + (far,):
            right_t = tie(rights[t], *swapped[-2:-1])
            rot = dot(right_t, rotated[0], (1, 0))
            for k in range(1, n_b):
                part = dot(right_t, rotated[k], (1, 0))
                swapped.append(across_b(part.astype(BF16), k))
                rot = rot + swapped[-1].astype(F32)
            rot = rot.astype(BF16)
            for q in range(n_b):
                block = (a - t) % n_a * n_b + q
                at = (block // per_row ^ r) * per_row + block % per_row
                rows = slice(q * sub, (q + 1) * sub)
                rot_k = lax.dynamic_update_index_in_dim(rot_k, rot[rows], at, 0)
                right_k = lax.dynamic_update_slice_in_dim(right_k, right_t[rows], at * sub, 0)

        step = moments_at if sub % 128 == 0 else moments_sliced
        rots = [rot_k[k * per_row : (k + 1) * per_row] for k in range(n_row)]
        rots[1:] = [across_rows(rots[k], k) for k in range(1, n_row)]

        kept, by_rows, held = (), [[] for _ in range(n_b)], []
        for k, rot in enumerate(rots):
            *kept, direction = step(r ^ k, n_row, sub, rot, first_moment, second_moment, tuple(kept))
            if k:
                direction = across_rows(direction, k)
            held.append(direction)
            if k:
                direction = jnp.concatenate(held, axis=1)
                held = []
                by_rows[0].append(direction)
                for q in range(1, n_b):
                    by_rows[q].append(across_b(direction, -q))
        first_new, second_new = kept
        by_rows = [jnp.concatenate(ds, axis=1) for ds in by_rows]
        direction = jnp.concatenate(by_rows, axis=0)

        def back(s, parts, kind):
            r_mine = lax.dynamic_slice_in_dim(right_k, n_at(s, core), half, 1)
            r_theirs = lax.dynamic_slice_in_dim(right_k, n_at(s, 1 - core), half, 1)
            w_mine, w_theirs = [], []
            for i, d in enumerate(parts):
                d_mine = d
                if i:
                    d, d_mine = tie(d, last["half"]), tie(d, last["rows"][-1])
                mine, theirs = half_sum(
                    dot(d, r_theirs, (1, 0)), dot(d_mine, r_mine, (1, 0)), 1
                )
                w_mine.append(mine)
                w_theirs.append(theirs)
            if len(parts) < n_b:
                w_mine, w_theirs = [
                    [w[0][k * own_i : (k + 1) * own_i] for k in range(n_b)] for w in (w_mine, w_theirs)
                ]
            return [product(list(zip(lefts, w)), kind) for w in (w_mine, w_theirs)]

        def joined(u):
            return jnp.concatenate(u, axis=1)

        def halves(x):
            return x[:, :half], x[:, half:]

        whole = [direction]
        passed = halves(a_shift(joined(back(2, by_rows, BF16)), 1))
        behind = halves(a_shift(joined(back(1, whole, BF16)), -1))
        ahead = [(u + x.astype(F32)).astype(BF16) for u, x in zip(back(3, whole, F32), passed)]
        ahead = halves(a_shift(joined(ahead), 1))
        own = back(0, whole, F32)
        u_mine, u_theirs = [
            (u + x.astype(F32) + y.astype(F32)).astype(BF16) for u, x, y in zip(own, behind, ahead)
        ]
        update = jnp.where(
            core == 0,
            jnp.concatenate([u_mine, u_theirs], axis=1),
            jnp.concatenate([u_theirs, u_mine], axis=1),
        )
        return update, first_new, second_new

    in_specs = (P("row", "col"), P("row", "col"), P("row", "col"), P("col", "row"), P("col", "row"))
    out_specs = (P("row", "col"), P("col", "row"), P("col", "row"))
    return jax.shard_map(per_device, mesh=mesh, in_specs=in_specs, out_specs=out_specs, check_vma=False)
```

```python
import functools

import jax
import jax.numpy as jnp
from jax import lax
from jax.experimental import pallas as pl
from jax.experimental.pallas import tpu as pltpu
from jax.sharding import PartitionSpec as P

BF16 = jnp.bfloat16
F32 = jnp.float32


def dot(a, b, contract):
    return lax.dot_general(a, b, ((contract[:1], contract[1:]), ((), ())), preferred_element_type=F32)


def tie(x, *earlier):
    return lax.optimization_barrier((x, *earlier))[0]


def product_kernel(n_pairs, *refs):
    out = refs[-1]
    total = None
    for x, y in zip(refs[:n_pairs], refs[n_pairs : 2 * n_pairs]):
        term = jnp.dot(x[...], y[...], preferred_element_type=F32)
        total = term if total is None else total + term
    for more in refs[2 * n_pairs : -1]:
        total = total + more[...].astype(F32)
    out[...] = total.astype(out.dtype)


def product(pairs, kind, more=(), by_rows=True):
    rows, columns = pairs[0][0].shape[0], pairs[0][1].shape[1]
    if by_rows:
        block = min(rows, 512)
        grid, out = rows // block, pl.BlockSpec((block, columns), lambda i: (i, 0))
        xs = [pl.BlockSpec((block, x.shape[1]), lambda i: (i, 0)) for x, _ in pairs]
        ys = [pl.BlockSpec(y.shape, lambda i: (0, 0)) for _, y in pairs]
    else:
        block = min(columns, 256)
        grid, out = columns // block, pl.BlockSpec((rows, block), lambda i: (0, i))
        xs = [pl.BlockSpec(x.shape, lambda i: (0, 0)) for x, _ in pairs]
        ys = [pl.BlockSpec((y.shape[0], block), lambda i: (0, i)) for _, y in pairs]
    return pl.pallas_call(
        functools.partial(product_kernel, len(pairs)),
        grid=(grid,),
        in_specs=xs + ys + [out] * len(more),
        out_specs=out,
        out_shape=jax.ShapeDtypeStruct((rows, columns), kind),
        cost_estimate=pl.CostEstimate(flops=512 * rows * columns, bytes_accessed=0, transcendentals=0),
        compiler_params=pltpu.CompilerParams(vmem_limit_bytes=16 * 2**20),
    )(*[x for x, _ in pairs], *[y for _, y in pairs], *more)


def moments(first, second, rot):
    first = 0.9 * first + 0.1 * rot
    second = 0.95 * second + 0.05 * rot * rot
    return first, second, (first / (jnp.sqrt(second) + 1e-08)).astype(BF16)


def moments_kernel(peer_ref, rot_ref, first_ref, second_ref, *refs):
    first_new, second_new, direction = refs[-3:]
    first_new[...], second_new[...], direction[...] = moments(
        first_ref[...], second_ref[...], rot_ref[0].astype(F32).T
    )


def moments_at(peer, n_row, sub, rot, first_moment, second_moment, before):
    blocks, _, rows = rot.shape
    block = min(rows, 512)
    packed_rot = pl.BlockSpec((1, sub, block), lambda q, i, p: (q, 0, i))
    at_peer = pl.BlockSpec((block, sub), lambda q, i, p: (i, q * n_row + p[0]))
    packed = pl.BlockSpec((block, sub), lambda q, i, p: (i, q))
    kept = [pl.BlockSpec(memory_space=pl.ANY)] * len(before)
    out = jax.ShapeDtypeStruct(first_moment.shape, F32)
    return pl.pallas_call(
        moments_kernel,
        grid_spec=pltpu.PrefetchScalarGridSpec(
            num_scalar_prefetch=1,
            grid=(blocks, rows // block),
            in_specs=[packed_rot, at_peer, at_peer] + kept,
            out_specs=[at_peer, at_peer, packed],
        ),
        out_shape=[out, out, jax.ShapeDtypeStruct((rows, blocks * sub), BF16)],
        input_output_aliases={4: 0, 5: 1} if before else {},
        compiler_params=pltpu.CompilerParams(vmem_limit_bytes=16 * 2**20),
        cost_estimate=pl.CostEstimate(
            flops=10 * rot.size, bytes_accessed=20 * rot.size, transcendentals=2 * rot.size
        ),
    )(peer.reshape(1), rot, first_moment, second_moment, *before)


def moments_sliced(peer, n_row, sub, rot, first_moment, second_moment, before):
    first_new, second_new = before if before else (first_moment, second_moment)
    directions = []
    for q in range(rot.shape[0]):
        start = (q * n_row + peer) * sub
        first, second, direction = moments(
            lax.dynamic_slice_in_dim(first_moment, start, sub, 1),
            lax.dynamic_slice_in_dim(second_moment, start, sub, 1),
            rot[q].astype(F32).T,
        )
        first_new = lax.dynamic_update_slice_in_dim(first_new, first, start, 1)
        second_new = lax.dynamic_update_slice_in_dim(second_new, second, start, 1)
        directions.append(direction)
    return first_new, second_new, jnp.concatenate(directions, axis=1)


def solution(mesh):
    n_row, n_col = mesh.shape["row"], mesh.shape["col"]
    n_a = 4
    n_b = n_col // n_a
    per_row = n_col // n_row

    def b_shift(x, db):
        perm = [(a * n_b + b, a * n_b + (b + db) % n_b) for a in range(n_a) for b in range(n_b)]
        return lax.ppermute(x, "col", perm)

    def a_shift(x, by):
        perm = [(a * n_b + b, (a + by) % n_a * n_b + b) for a in range(n_a) for b in range(n_b)]
        return lax.ppermute(x, "col", perm)

    def row_xor(x, k):
        return lax.ppermute(x, "row", [(r, r ^ k) for r in range(n_row)])

    def per_device(grad, basis_left, basis_right, first_moment, second_moment):
        last = {}

        def in_turn(link, x, move, depth):
            before = last.setdefault(link, [])
            if len(before) >= depth:
                x = tie(x, before[-depth])
            before.append(move(x))
            return before[-1]

        def across_b(x, k, depth=1):
            return in_turn("b", x, lambda y: b_shift(y, k), depth)

        def across_rows(x, k, depth=1):
            return row_xor(x, k) if k == 1 else in_turn("rows", x, lambda y: row_xor(y, k), depth)

        def half_sum(theirs, mine, depth):
            mine = (mine.astype(F32) + row_xor(theirs.astype(BF16), 1).astype(F32)).astype(BF16)
            last["half"] = mine
            k = 2
            while k < n_row:
                got = across_rows(mine, k, depth)
                mine = (mine.astype(F32) + got.astype(F32)).astype(BF16)
                k *= 2
            return mine, row_xor(mine, 1)

        r = lax.axis_index("row")
        c = lax.axis_index("col")
        a, b = c // n_b, c % n_b
        core = r % 2
        width = grad.shape[1]
        half = width // 2
        sub = width // n_row
        own_i = basis_left.shape[1]
        row_n = basis_right.shape[0]

        def n_at(s, h):
            return (a - s) % n_a * width + h * half

        grad = jnp.concatenate(
            [lax.dynamic_slice_in_dim(grad, h * half, half, 1).T for h in (core, 1 - core)], axis=0
        )
        grad = lax.optimization_barrier(grad)
        below, above = a_shift(grad, 1), a_shift(grad, -1)
        grads = [grad, below, a_shift(below, 1), above]

        own_left = tie(basis_left, grad)
        lefts = [own_left] + [across_b(own_left, -k) for k in range(1, n_b)]

        right_after = tie(basis_right, grad)
        right_n = jnp.zeros((sub, n_row * row_n), BF16)
        for k in range(n_row):
            part = lax.dynamic_slice_in_dim(right_after, (r ^ k) * sub, sub, 1).T
            if k:
                part = across_rows(part, k, 2)
            right_n = lax.dynamic_update_slice_in_dim(right_n, part, (r ^ k) * row_n, 1)
        by_b = right_n.reshape(sub, n_a, n_b, width)

        def rows_of(which):
            return lax.dynamic_index_in_dim(by_b, which, 2, keepdims=False).reshape(sub, n_a * width)

        got = [rows_of(b)] + [across_b(rows_of((b + k) % n_b), k, 2) for k in range(1, n_b)]
        stacked = jnp.stack(got, 0)
        right = [lax.dynamic_index_in_dim(stacked, (b - q) % n_b, 0, keepdims=False) for q in range(n_b)]
        right = jnp.concatenate(right, axis=0)

        near, far, last_b = (0, 1, 3), 2, n_b - 1
        turns = [(0, 0)] + [(k, s) for k in range(1, n_b) for s in near] + [(0, 1)]
        turns += [(k, far) for k in range(1, n_b)] + [(0, 3), (0, far)]
        rotated = [jnp.zeros((n_a * width, own_i), BF16) for _ in range(n_b)]
        for k, s in turns:
            if (k, s) == (1, 0):
                grads[1], grads[3], *lefts[1:] = tie((grads[1], grads[3], *lefts[1:]), right_n)
                sent = tie(right, grads[1], grads[3])
                below, above = a_shift(sent, 1), a_shift(sent, -1)
                rights = [right, below, a_shift(below, 1), above]
            if (k, s) == (1, 1):
                grads[1] = tie(grads[1], right)
            if (k, s) == (1, far):
                grads[far] = tie(grads[far], last["rows"][-2])
            g = tie(grads[s], rights[1], rights[3]) if (k, s) == (0, 3) else grads[s]
            term = product([(g, lefts[k])], BF16, by_rows=False)
            mine, theirs = half_sum(term[half:], term[:half], 1)
            rotated[k] = lax.dynamic_update_slice_in_dim(rotated[k], mine, n_at(s, core), 0)
            rotated[k] = lax.dynamic_update_slice_in_dim(rotated[k], theirs, n_at(s, 1 - core), 0)
        rot_k = jnp.zeros((n_col, sub, own_i), BF16)
        right_k = jnp.zeros((n_col * sub, n_a * width), BF16)
        swapped = []
        for t in near + (far,):
            right_t = tie(rights[t], *swapped[-2:-1], *(rights[2:3] if t == 1 else ()))
            rot = dot(right_t, rotated[0], (1, 0))
            for k in range(1, n_b):
                part = dot(right_t, rotated[k], (1, 0))
                swapped.append(across_b(part.astype(BF16), k))
                rot = rot + swapped[-1].astype(F32)
            rot = rot.astype(BF16)
            for q in range(n_b):
                block = (a - t) % n_a * n_b + q
                at = (block // per_row ^ r) * per_row + block % per_row
                rows = slice(q * sub, (q + 1) * sub)
                rot_k = lax.dynamic_update_index_in_dim(rot_k, rot[rows], at, 0)
                right_k = lax.dynamic_update_slice_in_dim(right_k, right_t[rows], at * sub, 0)

        step = moments_at if sub % 128 == 0 else moments_sliced
        rots = [rot_k[k * per_row : (k + 1) * per_row] for k in range(n_row)]
        rots[1:] = [across_rows(rots[k], k) for k in range(1, n_row)]

        kept, by_rows, held = (), [[] for _ in range(n_b)], []
        for k, rot in enumerate(rots):
            if k == n_row - 1:
                kept = tie(tuple(kept), by_rows[1][0])
            *kept, direction = step(r ^ k, n_row, sub, rot, first_moment, second_moment, tuple(kept))
            if k:
                direction = across_rows(direction, k)
            held.append(direction)
            if k:
                direction = jnp.concatenate(held, axis=1)
                held = []
                by_rows[0].append(direction)
                for q in range(1, n_b):
                    by_rows[q].append(across_b(direction, -q))
        first_new, second_new = kept
        by_rows = [jnp.concatenate(ds, axis=1) for ds in by_rows]
        direction = jnp.concatenate(by_rows, axis=0)

        def back(s, parts, kind, *arrived):
            r_mine = lax.dynamic_slice_in_dim(right_k, n_at(s, core), half, 1)
            r_theirs = lax.dynamic_slice_in_dim(right_k, n_at(s, 1 - core), half, 1)
            w_mine, w_theirs = [], []
            for i, d in enumerate(parts):
                d_mine = d
                if i:
                    d, d_mine = tie(d, last["half"]), tie(d, last["rows"][-1])
                mine, theirs = half_sum(
                    dot(d, r_theirs, (1, 0)), dot(d_mine, r_mine, (1, 0)), 1
                )
                w_mine.append(mine)
                w_theirs.append(theirs)
            if len(parts) < n_b:
                w_mine, w_theirs = [
                    [w[0][k * own_i : (k + 1) * own_i] for k in range(n_b)] for w in (w_mine, w_theirs)
                ]
            w_mine, w_theirs = tie((w_mine, w_theirs), *arrived)
            return [product(list(zip(lefts, w)), kind) for w in (w_mine, w_theirs)]

        def joined(u):
            return jnp.concatenate(u, axis=1)

        def halves(x):
            return x[:, :half], x[:, half:]

        whole = [direction]
        passed = halves(a_shift(joined(back(2, by_rows, BF16)), 1))
        behind = halves(a_shift(joined(back(1, whole, BF16)), -1))
        ahead = [(u + x.astype(F32)).astype(BF16) for u, x in zip(back(3, whole, F32, *passed), passed)]
        ahead = halves(a_shift(joined(ahead), 1))
        own = back(0, whole, F32)
        u_mine, u_theirs = [
            (u + x.astype(F32) + y.astype(F32)).astype(BF16) for u, x, y in zip(own, behind, ahead)
        ]
        update = jnp.where(
            core == 0,
            jnp.concatenate([u_mine, u_theirs], axis=1),
            jnp.concatenate([u_theirs, u_mine], axis=1),
        )
        return update, first_new, second_new

    in_specs = (P("row", "col"), P("row", "col"), P("row", "col"), P("col", "row"), P("col", "row"))
    out_specs = (P("row", "col"), P("col", "row"), P("col", "row"))
    return jax.shard_map(per_device, mesh=mesh, in_specs=in_specs, out_specs=out_specs, check_vma=False)
```

```python
import functools

import jax
import jax.numpy as jnp
from jax import lax
from jax.experimental import pallas as pl
from jax.experimental.pallas import tpu as pltpu
from jax.sharding import PartitionSpec as P

BF16 = jnp.bfloat16
F32 = jnp.float32


def dot(a, b, contract):
    return lax.dot_general(a, b, ((contract[:1], contract[1:]), ((), ())), preferred_element_type=F32)


def tie(x, *earlier):
    return lax.optimization_barrier((x, *earlier))[0]


def product_kernel(n_pairs, *refs):
    out = refs[-1]
    total = None
    for x, y in zip(refs[:n_pairs], refs[n_pairs : 2 * n_pairs]):
        term = jnp.dot(x[...], y[...], preferred_element_type=F32)
        total = term if total is None else total + term
    for more in refs[2 * n_pairs : -1]:
        total = total + more[...].astype(F32)
    out[...] = total.astype(out.dtype)


def product(pairs, kind, more=(), by_rows=True):
    rows, columns = pairs[0][0].shape[0], pairs[0][1].shape[1]
    if by_rows:
        block = min(rows, 512)
        grid, out = rows // block, pl.BlockSpec((block, columns), lambda i: (i, 0))
        xs = [pl.BlockSpec((block, x.shape[1]), lambda i: (i, 0)) for x, _ in pairs]
        ys = [pl.BlockSpec(y.shape, lambda i: (0, 0)) for _, y in pairs]
    else:
        block = min(columns, 256)
        grid, out = columns // block, pl.BlockSpec((rows, block), lambda i: (0, i))
        xs = [pl.BlockSpec(x.shape, lambda i: (0, 0)) for x, _ in pairs]
        ys = [pl.BlockSpec((y.shape[0], block), lambda i: (0, i)) for _, y in pairs]
    return pl.pallas_call(
        functools.partial(product_kernel, len(pairs)),
        grid=(grid,),
        in_specs=xs + ys + [out] * len(more),
        out_specs=out,
        out_shape=jax.ShapeDtypeStruct((rows, columns), kind),
        cost_estimate=pl.CostEstimate(flops=512 * rows * columns, bytes_accessed=0, transcendentals=0),
        compiler_params=pltpu.CompilerParams(vmem_limit_bytes=16 * 2**20),
    )(*[x for x, _ in pairs], *[y for _, y in pairs], *more)


def moments(first, second, rot):
    first = 0.9 * first + 0.1 * rot
    second = 0.95 * second + 0.05 * rot * rot
    return first, second, (first / (jnp.sqrt(second) + 1e-08)).astype(BF16)


def moments_kernel(peer_ref, rot_ref, first_ref, second_ref, *refs):
    first_new, second_new, direction = refs[-3:]
    first_new[...], second_new[...], direction[...] = moments(
        first_ref[...], second_ref[...], rot_ref[0].astype(F32).T
    )


def moments_at(peer, n_row, sub, rot, first_moment, second_moment, before):
    blocks, _, rows = rot.shape
    block = min(rows, 512)
    packed_rot = pl.BlockSpec((1, sub, block), lambda q, i, p: (q, 0, i))
    at_peer = pl.BlockSpec((block, sub), lambda q, i, p: (i, q * n_row + p[0]))
    packed = pl.BlockSpec((block, sub), lambda q, i, p: (i, q))
    kept = [pl.BlockSpec(memory_space=pl.ANY)] * len(before)
    out = jax.ShapeDtypeStruct(first_moment.shape, F32)
    return pl.pallas_call(
        moments_kernel,
        grid_spec=pltpu.PrefetchScalarGridSpec(
            num_scalar_prefetch=1,
            grid=(blocks, rows // block),
            in_specs=[packed_rot, at_peer, at_peer] + kept,
            out_specs=[at_peer, at_peer, packed],
        ),
        out_shape=[out, out, jax.ShapeDtypeStruct((rows, blocks * sub), BF16)],
        input_output_aliases={4: 0, 5: 1} if before else {},
        compiler_params=pltpu.CompilerParams(vmem_limit_bytes=16 * 2**20),
        cost_estimate=pl.CostEstimate(
            flops=10 * rot.size, bytes_accessed=20 * rot.size, transcendentals=2 * rot.size
        ),
    )(peer.reshape(1), rot, first_moment, second_moment, *before)


def moments_sliced(peer, n_row, sub, rot, first_moment, second_moment, before):
    first_new, second_new = before if before else (first_moment, second_moment)
    directions = []
    for q in range(rot.shape[0]):
        start = (q * n_row + peer) * sub
        first, second, direction = moments(
            lax.dynamic_slice_in_dim(first_moment, start, sub, 1),
            lax.dynamic_slice_in_dim(second_moment, start, sub, 1),
            rot[q].astype(F32).T,
        )
        first_new = lax.dynamic_update_slice_in_dim(first_new, first, start, 1)
        second_new = lax.dynamic_update_slice_in_dim(second_new, second, start, 1)
        directions.append(direction)
    return first_new, second_new, jnp.concatenate(directions, axis=1)


def solution(mesh):
    n_row, n_col = mesh.shape["row"], mesh.shape["col"]
    n_a = 4
    n_b = n_col // n_a
    per_row = n_col // n_row

    def b_shift(x, db):
        perm = [(a * n_b + b, a * n_b + (b + db) % n_b) for a in range(n_a) for b in range(n_b)]
        return lax.ppermute(x, "col", perm)

    def a_shift(x, by):
        perm = [(a * n_b + b, (a + by) % n_a * n_b + b) for a in range(n_a) for b in range(n_b)]
        return lax.ppermute(x, "col", perm)

    def row_xor(x, k):
        return lax.ppermute(x, "row", [(r, r ^ k) for r in range(n_row)])

    def per_device(grad, basis_left, basis_right, first_moment, second_moment):
        last = {}

        def in_turn(link, x, move, depth):
            before = last.setdefault(link, [])
            if len(before) >= depth:
                x = tie(x, before[-depth])
            before.append(move(x))
            return before[-1]

        def across_b(x, k, depth=1):
            return in_turn("b", x, lambda y: b_shift(y, k), depth)

        def across_rows(x, k, depth=1):
            return row_xor(x, k) if k == 1 else in_turn("rows", x, lambda y: row_xor(y, k), depth)

        def half_sum(theirs, mine, depth):
            mine = mine(row_xor(theirs(), 1))
            last["half"] = mine
            k = 2
            while k < n_row:
                got = across_rows(mine, k, depth)
                mine = (mine.astype(F32) + got.astype(F32)).astype(BF16)
                k *= 2
            return mine, row_xor(mine, 1)

        r = lax.axis_index("row")
        c = lax.axis_index("col")
        a, b = c // n_b, c % n_b
        core = r % 2
        width = grad.shape[1]
        half = width // 2
        sub = width // n_row
        own_i = basis_left.shape[1]
        row_n = basis_right.shape[0]

        def n_at(s, h):
            return (a - s) % n_a * width + h * half

        def halves(x):
            return x[:, :half], x[:, half:]

        grad = jnp.concatenate(
            [lax.dynamic_slice_in_dim(grad, h * half, half, 1).T for h in (core, 1 - core)], axis=0
        )
        grad = lax.optimization_barrier(grad)
        below, above = a_shift(grad, 1), a_shift(grad, -1)
        grads = [grad, below, a_shift(below, 1), above]

        own_left = tie(basis_left, grad)
        lefts = [own_left] + [across_b(own_left, -k) for k in range(1, n_b)]

        right_after = tie(basis_right, grad)
        right_n = jnp.zeros((sub, n_row * row_n), BF16)
        for k in range(n_row):
            part = lax.dynamic_slice_in_dim(right_after, (r ^ k) * sub, sub, 1).T
            if k:
                part = across_rows(part, k, 2)
            right_n = lax.dynamic_update_slice_in_dim(right_n, part, (r ^ k) * row_n, 1)
        by_b = right_n.reshape(sub, n_a, n_b, width)

        def rows_of(which):
            return lax.dynamic_index_in_dim(by_b, which, 2, keepdims=False).reshape(sub, n_a * width)

        got = [rows_of(b)] + [across_b(rows_of((b + k) % n_b), k) for k in range(1, n_b)]
        stacked = jnp.stack(got, 0)
        right = [lax.dynamic_index_in_dim(stacked, (b - q) % n_b, 0, keepdims=False) for q in range(n_b)]
        right = jnp.concatenate(right, axis=0)

        near, far, last_b = (0, 1, 3), 2, n_b - 1
        turns = [(0, 0)] + [(k, s) for k in range(1, n_b) for s in near] + [(0, 1)]
        turns += [(k, far) for k in range(1, n_b)] + [(0, 3), (0, far)]
        rotated = [jnp.zeros((n_a * width, own_i), BF16) for _ in range(n_b)]
        for k, s in turns:
            if (k, s) == (1, 0):
                grads[1], grads[3], *lefts[1:] = tie((grads[1], grads[3], *lefts[1:]), right_n)
                sent = tie(right, grads[1], grads[3])
                below, above = a_shift(sent, 1), a_shift(sent, -1)
                rights = [right, below, a_shift(below, 1), above]
            if (k, s) == (1, 1):
                grads[1] = tie(grads[1], right)
            if (k, s) == (1, far):
                grads[far] = tie(grads[far], last["rows"][-2])
            g = tie(grads[s], rights[2]) if (k, s) == turns[-1] else grads[s]
            g_mine, g_theirs = g[:half], g[half:]
            mine, theirs = half_sum(
                lambda: product([(g_theirs, lefts[k])], BF16, by_rows=False),
                lambda got: product([(g_mine, lefts[k])], BF16, (got,), by_rows=False),
                1,
            )
            rotated[k] = lax.dynamic_update_slice_in_dim(rotated[k], mine, n_at(s, core), 0)
            rotated[k] = lax.dynamic_update_slice_in_dim(rotated[k], theirs, n_at(s, 1 - core), 0)
        rot_k = jnp.zeros((n_col, sub, own_i), BF16)
        right_k = jnp.zeros((n_col * sub, n_a * width), BF16)
        swapped = []
        for t in near + (far,):
            right_t = tie(rights[t], *swapped[-2:-1])
            rot = dot(right_t, rotated[0], (1, 0))
            for k in range(1, n_b):
                part = dot(right_t, rotated[k], (1, 0))
                swapped.append(across_b(part.astype(BF16), k))
                rot = rot + swapped[-1].astype(F32)
            rot = rot.astype(BF16)
            for q in range(n_b):
                block = (a - t) % n_a * n_b + q
                at = (block // per_row ^ r) * per_row + block % per_row
                rows = slice(q * sub, (q + 1) * sub)
                rot_k = lax.dynamic_update_index_in_dim(rot_k, rot[rows], at, 0)
                right_k = lax.dynamic_update_slice_in_dim(right_k, right_t[rows], at * sub, 0)

        step = moments_at if sub % 128 == 0 else moments_sliced
        rots = [rot_k[k * per_row : (k + 1) * per_row] for k in range(n_row)]
        rots[1:] = [across_rows(rots[k], k, 2) for k in range(1, n_row)]

        kept, by_rows = (), [[] for _ in range(n_b)]
        for k, rot in enumerate(rots):
            if k == n_row - 1:
                kept = tie(tuple(kept), by_rows[1][1])
            *kept, direction = step(r ^ k, n_row, sub, rot, first_moment, second_moment, tuple(kept))
            if k:
                direction = across_rows(direction, k)
            by_rows[0].append(direction)
            for q in range(1, n_b):
                by_rows[q].append(across_b(direction, -q))
        first_new, second_new = kept
        by_rows = [jnp.concatenate(ds, axis=1) for ds in by_rows]
        direction = jnp.concatenate(by_rows, axis=0)

        def back(s, parts, kind):
            r_mine = lax.dynamic_slice_in_dim(right_k, n_at(s, core), half, 1)
            r_theirs = lax.dynamic_slice_in_dim(right_k, n_at(s, 1 - core), half, 1)
            w_mine, w_theirs = [], []
            for i, d in enumerate(parts):
                d_mine = d
                if i:
                    d, d_mine = tie(d, last["half"]), tie(d, last["rows"][-1])
                mine, theirs = half_sum(
                    lambda: dot(d, r_theirs, (1, 0)).astype(BF16),
                    lambda got: (dot(d_mine, r_mine, (1, 0)) + got.astype(F32)).astype(BF16),
                    1,
                )
                w_mine.append(mine)
                w_theirs.append(theirs)
            if len(parts) < n_b:
                w_mine, w_theirs = [
                    [w[0][k * own_i : (k + 1) * own_i] for k in range(n_b)] for w in (w_mine, w_theirs)
                ]
            return [product(list(zip(lefts, w)), kind) for w in (w_mine, w_theirs)]

        def joined(u):
            return jnp.concatenate(u, axis=1)

        whole = [direction]
        passed = halves(a_shift(joined(back(2, by_rows, BF16)), 1))
        behind = halves(a_shift(joined(back(1, whole, BF16)), -1))
        ahead = [(u + x.astype(F32)).astype(BF16) for u, x in zip(back(3, whole, F32), passed)]
        ahead = halves(a_shift(joined(ahead), 1))
        own = back(0, whole, F32)
        u_mine, u_theirs = [
            (u + x.astype(F32) + y.astype(F32)).astype(BF16) for u, x, y in zip(own, behind, ahead)
        ]
        update = jnp.where(
            core == 0,
            jnp.concatenate([u_mine, u_theirs], axis=1),
            jnp.concatenate([u_theirs, u_mine], axis=1),
        )
        return update, first_new, second_new

    in_specs = (P("row", "col"), P("row", "col"), P("row", "col"), P("col", "row"), P("col", "row"))
    out_specs = (P("row", "col"), P("col", "row"), P("col", "row"))
    return jax.shard_map(per_device, mesh=mesh, in_specs=in_specs, out_specs=out_specs, check_vma=False)
```

```python
import functools

import jax
import jax.numpy as jnp
from jax import lax
from jax.experimental import pallas as pl
from jax.experimental.pallas import tpu as pltpu
from jax.sharding import PartitionSpec as P

BF16 = jnp.bfloat16
F32 = jnp.float32


def dot(a, b, contract):
    return lax.dot_general(a, b, ((contract[:1], contract[1:]), ((), ())), preferred_element_type=F32)


def tie(x, *earlier):
    return lax.optimization_barrier((x, *earlier))[0]


def product_kernel(n_pairs, *refs):
    out = refs[-1]
    total = None
    for x, y in zip(refs[:n_pairs], refs[n_pairs : 2 * n_pairs]):
        term = jnp.dot(x[...], y[...], preferred_element_type=F32)
        total = term if total is None else total + term
    for more in refs[2 * n_pairs : -1]:
        total = total + more[...].astype(F32)
    out[...] = total.astype(out.dtype)


def product(pairs, kind, more=(), by_rows=True):
    rows, columns = pairs[0][0].shape[0], pairs[0][1].shape[1]
    if by_rows:
        block = min(rows, 512)
        grid, out = rows // block, pl.BlockSpec((block, columns), lambda i: (i, 0))
        xs = [pl.BlockSpec((block, x.shape[1]), lambda i: (i, 0)) for x, _ in pairs]
        ys = [pl.BlockSpec(y.shape, lambda i: (0, 0)) for _, y in pairs]
    else:
        block = min(columns, 256)
        grid, out = columns // block, pl.BlockSpec((rows, block), lambda i: (0, i))
        xs = [pl.BlockSpec(x.shape, lambda i: (0, 0)) for x, _ in pairs]
        ys = [pl.BlockSpec((y.shape[0], block), lambda i: (0, i)) for _, y in pairs]
    return pl.pallas_call(
        functools.partial(product_kernel, len(pairs)),
        grid=(grid,),
        in_specs=xs + ys + [out] * len(more),
        out_specs=out,
        out_shape=jax.ShapeDtypeStruct((rows, columns), kind),
        cost_estimate=pl.CostEstimate(flops=512 * rows * columns, bytes_accessed=0, transcendentals=0),
        compiler_params=pltpu.CompilerParams(vmem_limit_bytes=16 * 2**20),
    )(*[x for x, _ in pairs], *[y for _, y in pairs], *more)


def moments(first, second, rot):
    first = 0.9 * first + 0.1 * rot
    second = 0.95 * second + 0.05 * rot * rot
    return first, second, (first / (jnp.sqrt(second) + 1e-08)).astype(BF16)


def moments_kernel(peer_ref, rot_ref, first_ref, second_ref, *refs):
    first_new, second_new, direction = refs[-3:]
    first_new[...], second_new[...], direction[...] = moments(
        first_ref[...], second_ref[...], rot_ref[0].astype(F32).T
    )


def moments_at(peer, n_row, sub, rot, first_moment, second_moment, before):
    blocks, _, rows = rot.shape
    block = min(rows, 512)
    packed_rot = pl.BlockSpec((1, sub, block), lambda q, i, p: (q, 0, i))
    at_peer = pl.BlockSpec((block, sub), lambda q, i, p: (i, q * n_row + p[0]))
    packed = pl.BlockSpec((block, sub), lambda q, i, p: (i, q))
    kept = [pl.BlockSpec(memory_space=pl.ANY)] * len(before)
    out = jax.ShapeDtypeStruct(first_moment.shape, F32)
    return pl.pallas_call(
        moments_kernel,
        grid_spec=pltpu.PrefetchScalarGridSpec(
            num_scalar_prefetch=1,
            grid=(blocks, rows // block),
            in_specs=[packed_rot, at_peer, at_peer] + kept,
            out_specs=[at_peer, at_peer, packed],
        ),
        out_shape=[out, out, jax.ShapeDtypeStruct((rows, blocks * sub), BF16)],
        input_output_aliases={4: 0, 5: 1} if before else {},
        compiler_params=pltpu.CompilerParams(vmem_limit_bytes=16 * 2**20),
        cost_estimate=pl.CostEstimate(
            flops=10 * rot.size, bytes_accessed=20 * rot.size, transcendentals=2 * rot.size
        ),
    )(peer.reshape(1), rot, first_moment, second_moment, *before)


def moments_sliced(peer, n_row, sub, rot, first_moment, second_moment, before):
    first_new, second_new = before if before else (first_moment, second_moment)
    directions = []
    for q in range(rot.shape[0]):
        start = (q * n_row + peer) * sub
        first, second, direction = moments(
            lax.dynamic_slice_in_dim(first_moment, start, sub, 1),
            lax.dynamic_slice_in_dim(second_moment, start, sub, 1),
            rot[q].astype(F32).T,
        )
        first_new = lax.dynamic_update_slice_in_dim(first_new, first, start, 1)
        second_new = lax.dynamic_update_slice_in_dim(second_new, second, start, 1)
        directions.append(direction)
    return first_new, second_new, jnp.concatenate(directions, axis=1)


def solution(mesh):
    n_row, n_col = mesh.shape["row"], mesh.shape["col"]
    n_a = 4
    n_b = n_col // n_a
    per_row = n_col // n_row

    def b_shift(x, db):
        perm = [(a * n_b + b, a * n_b + (b + db) % n_b) for a in range(n_a) for b in range(n_b)]
        return lax.ppermute(x, "col", perm)

    def a_shift(x, by):
        perm = [(a * n_b + b, (a + by) % n_a * n_b + b) for a in range(n_a) for b in range(n_b)]
        return lax.ppermute(x, "col", perm)

    def row_xor(x, k):
        return lax.ppermute(x, "row", [(r, r ^ k) for r in range(n_row)])

    def per_device(grad, basis_left, basis_right, first_moment, second_moment):
        last = {}

        def in_turn(link, x, move, depth):
            before = last.setdefault(link, [])
            if len(before) >= depth:
                x = tie(x, before[-depth])
            before.append(move(x))
            return before[-1]

        def across_b(x, k, depth=1):
            return in_turn("b", x, lambda y: b_shift(y, k), depth)

        def across_rows(x, k, depth=1):
            return row_xor(x, k) if k == 1 else in_turn("rows", x, lambda y: row_xor(y, k), depth)

        def half_sum(theirs, mine, depth):
            mine = mine(row_xor(theirs(), 1))
            last["half"] = mine
            k = 2
            while k < n_row:
                got = across_rows(mine, k, depth)
                mine = (mine.astype(F32) + got.astype(F32)).astype(BF16)
                k *= 2
            return mine, row_xor(mine, 1)

        r = lax.axis_index("row")
        c = lax.axis_index("col")
        a, b = c // n_b, c % n_b
        core = r % 2
        width = grad.shape[1]
        half = width // 2
        sub = width // n_row
        own_i = basis_left.shape[1]
        row_n = basis_right.shape[0]

        def n_at(s, h):
            return (a - s) % n_a * width + h * half

        def halves(x):
            return x[:, :half], x[:, half:]

        grad = jnp.concatenate(
            [lax.dynamic_slice_in_dim(grad, h * half, half, 1).T for h in (core, 1 - core)], axis=0
        )
        grad = lax.optimization_barrier(grad)
        below, above = a_shift(grad, 1), a_shift(grad, -1)
        grads = [grad, below, a_shift(below, 1), above]

        own_left = tie(basis_left, grad)
        lefts = [own_left] + [across_b(own_left, -k) for k in range(1, n_b)]

        right_after = tie(basis_right, grad)
        right_n = jnp.zeros((sub, n_row * row_n), BF16)
        for k in range(n_row):
            part = lax.dynamic_slice_in_dim(right_after, (r ^ k) * sub, sub, 1).T
            if k:
                part = across_rows(part, k, 2)
            right_n = lax.dynamic_update_slice_in_dim(right_n, part, (r ^ k) * row_n, 1)
        by_b = right_n.reshape(sub, n_a, n_b, width)

        def rows_of(which):
            return lax.dynamic_index_in_dim(by_b, which, 2, keepdims=False).reshape(sub, n_a * width)

        got = [rows_of(b)] + [across_b(rows_of((b + k) % n_b), k) for k in range(1, n_b)]
        stacked = jnp.stack(got, 0)
        right = [lax.dynamic_index_in_dim(stacked, (b - q) % n_b, 0, keepdims=False) for q in range(n_b)]
        right = jnp.concatenate(right, axis=0)

        near, far, last_b = (0, 1, 3), 2, n_b - 1
        turns = [(0, 0)] + [(k, s) for k in range(1, n_b) for s in near] + [(0, 1)]
        turns += [(k, far) for k in range(1, n_b)] + [(0, 3), (0, far)]
        rotated = [jnp.zeros((n_a * width, own_i), BF16) for _ in range(n_b)]
        for k, s in turns:
            if (k, s) == (1, 0):
                grads[1], grads[3], *lefts[1:] = tie((grads[1], grads[3], *lefts[1:]), right_n)
                sent = tie(right, grads[1], grads[3])
                below, above = a_shift(sent, 1), a_shift(sent, -1)
                rights = [right, below, a_shift(below, 1), above]
            if (k, s) == (1, 1):
                grads[1] = tie(grads[1], right)
            if (k, s) == (1, far):
                grads[far] = tie(grads[far], last["rows"][-2])
            g = tie(grads[s], rights[2], rights[3]) if (k, s) == turns[-1] else grads[s]
            g_mine, g_theirs = g[:half], g[half:]
            mine, theirs = half_sum(
                lambda: product([(g_theirs, lefts[k])], BF16, by_rows=False),
                lambda got: product([(g_mine, lefts[k])], BF16, (got,), by_rows=False),
                1,
            )
            rotated[k] = lax.dynamic_update_slice_in_dim(rotated[k], mine, n_at(s, core), 0)
            rotated[k] = lax.dynamic_update_slice_in_dim(rotated[k], theirs, n_at(s, 1 - core), 0)
        rot_k = jnp.zeros((n_col, sub, own_i), BF16)
        right_k = jnp.zeros((n_col * sub, n_a * width), BF16)
        swapped = []
        for t in near + (far,):
            right_t = tie(rights[t], *swapped[-2:-1])
            rot = dot(right_t, rotated[0], (1, 0))
            for k in range(1, n_b):
                part = dot(right_t, rotated[k], (1, 0))
                swapped.append(across_b(part.astype(BF16), k))
                rot = rot + swapped[-1].astype(F32)
            rot = rot.astype(BF16)
            for q in range(n_b):
                block = (a - t) % n_a * n_b + q
                at = (block // per_row ^ r) * per_row + block % per_row
                rows = slice(q * sub, (q + 1) * sub)
                rot_k = lax.dynamic_update_index_in_dim(rot_k, rot[rows], at, 0)
                right_k = lax.dynamic_update_slice_in_dim(right_k, right_t[rows], at * sub, 0)

        step = moments_at if sub % 128 == 0 else moments_sliced
        rots = [rot_k[k * per_row : (k + 1) * per_row] for k in range(n_row)]
        rots[1:] = [across_rows(rots[k], k, 2) for k in range(1, n_row)]

        kept, by_rows = (), [[] for _ in range(n_b)]
        for k, rot in enumerate(rots):
            if k == n_row - 1:
                kept = tie(tuple(kept), by_rows[1][0])
            *kept, direction = step(r ^ k, n_row, sub, rot, first_moment, second_moment, tuple(kept))
            if k:
                direction = across_rows(direction, k)
            by_rows[0].append(direction)
            for q in range(1, n_b):
                by_rows[q].append(across_b(direction, -q))
        first_new, second_new = kept
        by_rows = [jnp.concatenate(ds, axis=1) for ds in by_rows]
        direction = jnp.concatenate(by_rows, axis=0)

        def back(s, parts, kind):
            r_mine = lax.dynamic_slice_in_dim(right_k, n_at(s, core), half, 1)
            r_theirs = lax.dynamic_slice_in_dim(right_k, n_at(s, 1 - core), half, 1)
            w_mine, w_theirs = [], []
            for i, d in enumerate(parts):
                d_mine = d
                if i:
                    d, d_mine = tie(d, last["half"]), tie(d, last["rows"][-1])
                mine, theirs = half_sum(
                    lambda: dot(d, r_theirs, (1, 0)).astype(BF16),
                    lambda got: (dot(d_mine, r_mine, (1, 0)) + got.astype(F32)).astype(BF16),
                    1,
                )
                w_mine.append(mine)
                w_theirs.append(theirs)
            if len(parts) < n_b:
                w_mine, w_theirs = [
                    [w[0][k * own_i : (k + 1) * own_i] for k in range(n_b)] for w in (w_mine, w_theirs)
                ]
            return [product(list(zip(lefts, w)), kind) for w in (w_mine, w_theirs)]

        def joined(u):
            return jnp.concatenate(u, axis=1)

        whole = [direction]
        passed = halves(a_shift(joined(back(2, by_rows, BF16)), 1))
        behind = halves(a_shift(joined(back(1, whole, BF16)), -1))
        ahead = [(u + x.astype(F32)).astype(BF16) for u, x in zip(back(3, whole, F32), passed)]
        ahead = halves(a_shift(joined(ahead), 1))
        own = back(0, whole, F32)
        u_mine, u_theirs = [
            (u + x.astype(F32) + y.astype(F32)).astype(BF16) for u, x, y in zip(own, behind, ahead)
        ]
        update = jnp.where(
            core == 0,
            jnp.concatenate([u_mine, u_theirs], axis=1),
            jnp.concatenate([u_theirs, u_mine], axis=1),
        )
        return update, first_new, second_new

    in_specs = (P("row", "col"), P("row", "col"), P("row", "col"), P("col", "row"), P("col", "row"))
    out_specs = (P("row", "col"), P("col", "row"), P("col", "row"))
    return jax.shard_map(per_device, mesh=mesh, in_specs=in_specs, out_specs=out_specs, check_vma=False)
```
